128 devices in a mesh: blk: 16 (over z, x_hi, core), group: 8 (over y, x_lo).
Axes of the slice: x: 4 (x_hi: 2, x_lo: 2; x = x_hi * 2 + x_lo), y: 4, z: 4, core: 2. Of those that a mesh axis runs over, the one named last changes fastest.
Arguments:
- images: bfloat16 [22528, 1152], P(('blk', 'group')), may hold values from -0.1796875 to 0.1796875
- texts: bfloat16 [22528, 1152], P(('blk', 'group')), may hold values from -0.1796875 to 0.1796875
- match: int32 [22528], P(('blk', 'group')), may hold values from 0 to 22527, each once
- logit_scale: float32 [1], replicated, may hold values from 20 to 40
- logit_bias: float32 [1], replicated, may hold values from -7 to -4
Outputs:
- image_grad: float32 [22528, 1152], P(('blk', 'group'))
- text_grad: float32 [22528, 1152], P(('blk', 'group'))
The draws below stay inside these ranges and needn't reach their ends.
Inputs may be any that keep to these rules, and one draw needn't show every extreme that they name: match holds each text index exactly once.
All inputs are finite; a program needn't handle non-finite values.
Results may differ from the reference program's by a relative error of at most 0.008.
Values may be sent and summed in bfloat16 or wider, within the bound.
A program may use at most 128 MiB of HBM per device.

```python
import jax
import jax.numpy as jnp
from jax import lax

D = 1152
TOKENS = 22528
N_BLK = 16
N_GROUP = 8


def levels(own_key, shape, pieces, smallest, high):
    loudness = 1.0
    for axis_at, blocks in pieces:
        heights = jax.random.uniform(jax.random.fold_in(jax.random.fold_in(own_key, 6), axis_at), (blocks,), jnp.float32, smallest / len(pieces), high / len(pieces))
        loudness = loudness * jnp.repeat(jnp.exp(heights), shape[axis_at] // blocks).reshape((-1,) + (1,) * (len(shape) - 1 - axis_at))
    return loudness


def bell_draw(stream_key, dims, scale, reach, shards=(), kind=jnp.bfloat16):
    loudness = levels(stream_key, dims, shards, -0.22, 0.18) if shards else 1.0
    array = jax.random.normal(stream_key, dims, jnp.float32) * scale * loudness
    return jnp.minimum(jnp.maximum(array, -reach), reach).astype(kind)


def setup_inputs(seed: int = 0) -> dict:
    splits = jax.random.split(jax.random.key(seed), 6)
    images = bell_draw(splits[0], (TOKENS, D), 0.03, 0.1796875, ((0, 128),))
    texts = bell_draw(splits[1], (TOKENS, D), 0.03, 0.1796875, ((0, 128),))
    match = jax.random.permutation(splits[2], TOKENS).astype(jnp.int32)
    logit_scale = jnp.clip(jax.random.uniform(splits[3], (1,), jnp.float32, 20.0, 40.0), 20.0, 40.0)
    logit_bias = jnp.clip(jax.random.uniform(splits[4], (1,), jnp.float32, -7.0, -4.0), -7.0, -4.0)
    return {"images": images, "texts": texts, "match": match, "logit_scale": logit_scale, "logit_bias": logit_bias}


epsilon = 1e-06

def unit_rows(x):
    values = x.astype(jnp.float32)
    scale = lax.rsqrt(lax.optimization_barrier(jnp.sum(values * values, axis=1, keepdims=True)) + epsilon)
    return (values * scale, scale)

def norm_back(unit, scale, grad):
    inner = lax.optimization_barrier(jnp.sum(unit * grad, axis=1, keepdims=True))
    return scale * (grad - unit * inner)

def rounded(x):
    low = lax.optimization_barrier(x.astype(jnp.bfloat16))
    return low.astype(jnp.float32)

def reference(images, texts, match, logit_scale, logit_bias):
    image_unit, image_scale = unit_rows(images)
    text_unit, text_scale = unit_rows(texts)
    image_send = rounded(image_unit)
    text_send = rounded(text_unit)
    factor = logit_scale[0]
    offset = logit_bias[0]
    block_rows = TOKENS // (N_BLK * N_GROUP) * N_GROUP
    block_count = TOKENS // block_rows
    columns = jnp.arange(TOKENS, dtype=jnp.int32)
    highest = lax.Precision.HIGHEST

    def image_step(text_total, block_index):
        first_row = (block_index * block_rows).astype(jnp.int32)
        image_block = lax.dynamic_slice_in_dim(image_send, first_row, block_rows, 0)
        match_block = lax.dynamic_slice_in_dim(match, first_row, block_rows, 0)
        logits = factor * jnp.dot(image_block, text_send.T, precision=highest) + offset
        positive = match_block[:, None] == columns[None, :]
        weight = jnp.where(positive, -jax.nn.sigmoid(-logits), jax.nn.sigmoid(logits))
        weight = rounded(weight)
        image_part = factor * jnp.dot(weight, text_send, precision=highest)
        text_total = text_total + factor * jnp.dot(weight.T, image_block, precision=highest)
        return (text_total, image_part)
    start_total = jnp.zeros((TOKENS, D), jnp.float32)
    text_total, image_parts = lax.scan(image_step, start_total, jnp.arange(block_count, dtype=jnp.int32))
    image_total = image_parts.reshape(TOKENS, D)
    image_grad = norm_back(image_unit, image_scale, image_total)
    text_grad = norm_back(text_unit, text_scale, text_total)
    return (image_grad, text_grad)
```

```python
import jax
import jax.numpy as jnp
from jax import lax
from jax.experimental import pallas as pl
from jax.experimental.pallas import tpu as pltpu
from jax.sharding import PartitionSpec as P

epsilon = 1e-06
MESH = pl.DeviceIdType.MESH
ROWS, WIDTH = 176, 1152
CUT, HALF_A, HALF_B = 80, 48, 128
A, B = (0, CUT), (CUT, ROWS)
A0, A1, B0, B1 = (0, HALF_A), (HALF_A, CUT), (CUT, HALF_B), (HALF_B, ROWS)
IMAGES, TEXTS = 8 * ROWS, 16 * ROWS
CHUNK = 4 * ROWS
SEMS = 96
bf16, f32 = jnp.bfloat16, jnp.float32


def place():
    b, g = lax.axis_index("blk"), lax.axis_index("group")
    x = lax.rem(b // 2, 2) * 2 + lax.rem(g, 2)
    return x, g // 2, b // 4, lax.rem(b, 2)


def device(x, y, z, core):
    return ((z * 2 + x // 2) * 2 + core, y * 2 + lax.rem(x, 2))


def unit_rows(x):
    values = x.astype(f32)
    scale = lax.rsqrt(jnp.sum(values * values, axis=1, keepdims=True) + epsilon)
    return values * scale, scale


def norm_back(x, grad):
    unit, scale = unit_rows(x)
    inner = jnp.sum(unit * grad, axis=1, keepdims=True)
    return scale * (grad - unit * inner)


class Links:
    def __init__(self, send_sems, recv_sems):
        self.send_sems, self.recv_sems = send_sems, recv_sems
        self.copies, self.sent = {}, 0

    def send(self, name, src, dst, target):
        k = len(self.copies)
        copy = pltpu.make_async_remote_copy(
            src_ref=src, dst_ref=dst, send_sem=self.send_sems.at[k], recv_sem=self.recv_sems.at[k],
            device_id=target, device_id_type=MESH,
        )
        copy.start()
        self.copies[name] = copy

    def arrived(self, *names):
        for name in names:
            self.copies[name].wait_recv()

    def finish(self):
        for copy in list(self.copies.values())[self.sent :]:
            copy.wait_send()
        self.sent = len(self.copies)


class Side:
    def __init__(self, tag, links, up, down, partner, slots, offset):
        self.tag, self.links, self.up, self.down, self.partner = tag, links, up, down, partner
        self.slots, self.offset = slots, offset

    def at(self, ref, r, p, rows):
        return ref.at[pl.ds(self.offset(r, p) + rows[0], rows[1] - rows[0])]

    def send(self, name, src, dst, target):
        self.links.send(self.tag + name, src, dst, target)

    def arrived(self, *names):
        self.links.arrived(*(self.tag + n for n in names))

    def gather_start(self):
        at, s = self.at, self.slots
        self.send("gB", at(s, 0, 0, B), at(s, 0, 1, B), self.partner)
        self.send("gA3", at(s, 0, 0, A), at(s, 3, 0, A), self.up)
        self.send("gA1", at(s, 0, 0, A), at(s, 1, 0, A), self.down)
        self.send("gB3", at(s, 0, 0, B), at(s, 3, 0, B), self.up)
        self.send("gB1", at(s, 0, 0, B), at(s, 1, 0, B), self.down)
        self.send("gA", at(s, 0, 0, A), at(s, 0, 1, A), self.partner)

    def gather_pair(self):
        at, s = self.at, self.slots
        self.arrived("gB")
        self.send("gC3", at(s, 0, 1, B), at(s, 3, 1, B), self.up)
        self.send("gC1", at(s, 0, 1, B), at(s, 1, 1, B), self.down)

    def gather_a(self):
        at, s = self.at, self.slots
        self.arrived("gA1", "gA3")
        self.send("gA20", at(s, 1, 0, A0), at(s, 2, 0, A0), self.down)
        self.send("gA21", at(s, 3, 0, A1), at(s, 2, 0, A1), self.up)
        self.send("gD1", at(s, 1, 0, A), at(s, 1, 1, A), self.partner)
        self.send("gD3", at(s, 3, 0, A), at(s, 3, 1, A), self.partner)

    def gather_b(self):
        at, s = self.at, self.slots
        self.arrived("gB1", "gB3")
        self.send("gB20", at(s, 1, 0, B0), at(s, 2, 0, B0), self.down)
        self.send("gB21", at(s, 3, 0, B1), at(s, 2, 0, B1), self.up)

    def gather_a2(self):
        at, s = self.at, self.slots
        self.arrived("gA20", "gA21")
        self.send("gD2", at(s, 2, 0, A), at(s, 2, 1, A), self.partner)

    def gather_c(self):
        at, s = self.at, self.slots
        self.arrived("gC1", "gC3")
        self.send("gC20", at(s, 1, 1, B0), at(s, 2, 1, B0), self.down)
        self.send("gC21", at(s, 3, 1, B1), at(s, 2, 1, B1), self.up)

    def sum_refs(self, pair_a, half, ring):
        self.pair_a, self.half, self.ring = pair_a, half, ring

    def rows_of(self, r, p, rows):
        return pl.ds(self.offset(r, p) + rows[0], rows[1] - rows[0])

    def mine(self, r, p, rows):
        return self.slots.at[self.rows_of(r, p, rows)]

    def pair_slot(self, r):
        return pl.ds(r * CUT, CUT)

    def half_slot(self, kind, rows):
        base = 0 if kind == 0 else CUT + (kind - 1) * (ROWS - CUT) - CUT
        return pl.ds(base + rows[0], rows[1] - rows[0])

    def ring_slot(self, r, p, rows):
        return pl.ds((r * 2 + p) * ROWS + rows[0], rows[1] - rows[0])

    def add(self, rows, *pieces):
        total = self.slots[rows, :].astype(f32)
        for ref, where in pieces:
            total = total + ref[where, :].astype(f32)
        self.slots[rows, :] = total.astype(bf16)

    def sum_far(self):
        self.send("sX2", self.mine(2, 1, A), self.pair_a.at[self.pair_slot(2)], self.partner)
        for p in (0, 1):
            self.send(f"sH0{p}", self.mine(2, p, B0), self.half.at[self.half_slot(1 + p, B0)], self.up)
            self.send(f"sH1{p}", self.mine(2, p, B1), self.half.at[self.half_slot(1 + p, B1)], self.down)

    def sum_far_a(self):
        self.arrived("sX2")
        self.add(self.rows_of(2, 0, A), (self.pair_a, self.pair_slot(2)))
        self.send("sHA0", self.mine(2, 0, A0), self.half.at[self.half_slot(0, A0)], self.up)
        self.send("sHA1", self.mine(2, 0, A1), self.half.at[self.half_slot(0, A1)], self.down)

    def sum_near(self, r):
        h, rows, target, slot = ("0", B0, self.up, 0) if r == 1 else ("1", B1, self.down, 1)
        self.send(f"sX{r}", self.mine(r, 1, A), self.pair_a.at[self.pair_slot(r)], self.partner)
        for p in (0, 1):
            self.arrived(f"sH{h}{p}")
            self.add(self.rows_of(r, p, rows), (self.half, self.half_slot(1 + p, rows)))
            self.send(f"sR{r}{p}", self.mine(r, p, B), self.ring.at[self.ring_slot(slot, p, B)], target)

    def sum_near_a(self, r):
        h, rows, target, slot = ("0", A0, self.up, 0) if r == 1 else ("1", A1, self.down, 1)
        self.arrived(f"sX{r}", f"sHA{h}")
        self.add(self.rows_of(r, 0, A), (self.pair_a, self.pair_slot(r)))
        self.add(self.rows_of(r, 0, rows), (self.half, self.half_slot(0, rows)))
        self.send(f"sRA{r}", self.mine(r, 0, A), self.ring.at[self.ring_slot(slot, 0, A)], target)

    def sum_own(self):
        self.send("sX0", self.mine(0, 1, A), self.pair_a.at[self.pair_slot(0)], self.partner)

    def sum_own_b(self):
        self.arrived("sR11", "sR31")
        self.add(self.rows_of(0, 1, B), (self.ring, self.ring_slot(0, 1, B)), (self.ring, self.ring_slot(1, 1, B)))
        self.send("sXB", self.mine(0, 1, B), self.pair_a.at[pl.ds(4 * CUT, ROWS - CUT)], self.partner)

    def total(self, own):
        self.arrived("sX0", "sRA1", "sRA3", "sR10", "sR30", "sXB")
        rest = self.ring[self.ring_slot(0, 0, (0, ROWS)), :].astype(f32)
        rest = rest + self.ring[self.ring_slot(1, 0, (0, ROWS)), :].astype(f32)
        first = self.pair_a[self.pair_slot(0), :].astype(f32)
        last = self.pair_a[pl.ds(4 * CUT, ROWS - CUT), :].astype(f32)
        return own + rest + jnp.concatenate([first, last], axis=0)


def dot(a, b, ca, cb):
    return lax.dot_general(a, b, (((ca,), (cb,)), ((), ())), preferred_element_type=f32)


def kernel(
    images, texts, matches, scale_ref, bias_ref, image_grad, text_grad,
    i_slots, t_slots, m_slots, where_ref, di, dt, t_sib,
    i_pair, t_pair, i_half, t_half, i_ring, t_ring, send_sems, recv_sems,
):
    x, y, z, core = place()
    odd = lax.rem(x, 2)
    xi = x + 1 - 2 * odd
    xt = lax.rem(x + 3 + 2 * odd, 4)
    y_up, y_down, y_far = lax.rem(y + 1, 4), lax.rem(y + 3, 4), lax.rem(y + 2, 4)
    z_up, z_down = lax.rem(z + 1, 4), lax.rem(z + 3, 4)
    sibling = device(x, y, z, 1 - core)
    peers = {(r, p): device((x, xi)[p], (y, y_up, y_far, y_down)[r], z, core) for r in range(4) for p in range(2)}
    up_t, down_t = device(x, y, z_up, core), device(x, y, z_down, core)
    pair_t = device(xt, y, z, core)

    barrier = pltpu.get_barrier_semaphore()
    greeted = [d for k, d in peers.items() if k != (0, 0)] + [up_t, down_t, pair_t, sibling]
    for d in greeted:
        pl.semaphore_signal(barrier, inc=1, device_id=d, device_id_type=MESH)
    i_slots[pl.ds(0, ROWS), :] = unit_rows(images[...])[0].astype(bf16)
    t_slots[pl.ds(0, ROWS), :] = unit_rows(texts[...])[0].astype(bf16)
    m_slots[0] = matches[0]
    pl.semaphore_wait(barrier, len(greeted))

    links = Links(send_sems, recv_sems)
    im = Side("i", links, peers[1, 0], peers[3, 0], peers[0, 1], i_slots, lambda r, p: (r * 2 + p) * ROWS)
    te = Side("t", links, up_t, down_t, pair_t, t_slots, lambda r, p: (r * 4 + p) * ROWS)
    im.sum_refs(i_pair, i_half, i_ring)
    te.sum_refs(t_pair, t_half, t_ring)
    both = (im, te)

    def to_sibling(r):
        links.send(f"sib{r}", t_slots.at[pl.ds(r * CHUNK, 2 * ROWS)], t_slots.at[pl.ds(r * CHUNK + 2 * ROWS, 2 * ROWS)], sibling)

    for side in both:
        side.gather_start()
    for r in range(4):
        for p in range(2):
            if (r, p) != (0, 0):
                k = ((4 - r) % 4) * 2 + p
                links.send(f"m{k}", matches.at[k], m_slots.at[k], peers[r, p])
    for side in both:
        side.gather_pair()
    for side in both:
        side.gather_a()
    for side in both:
        side.gather_b()
    te.arrived("gA")
    to_sibling(0)
    for side in both:
        side.gather_a2()
    for side in both:
        side.gather_c()

    links.arrived(*(f"m{k}" for k in range(1, 8)))
    match = m_slots[0]
    for k in range(1, 8):
        match = match + m_slots[k]
    owner = ((match.astype(f32) + 0.5) * (1.0 / ROWS)).astype(jnp.int32)
    b, g = owner >> 3, owner & 7
    ox = ((b >> 1) & 1) * 2 + (g & 1)
    held = ((g >> 1) == y) & ((ox == x) | (ox == xt))
    slot = (((b >> 2) - z + 4) & 3) * 4 + jnp.where((b & 1) == core, 0, 2) + jnp.where(ox == x, 0, 1)
    where_ref[...] = jnp.where(held, slot * ROWS + match - owner * ROWS, -1)

    im.arrived("gA", "gD1", "gD3")
    te.arrived("gD1", "gD3")
    to_sibling(1)
    to_sibling(3)
    for side in both:
        side.arrived("gB20", "gB21", "gC20", "gC21", "gD2")
    to_sibling(2)

    factor, bias = scale_ref[0], bias_ref[0]

    def block(r, first):
        t = t_slots[pl.ds(r * CHUNK, CHUNK), :]
        i = i_slots[...]
        logits = factor * dot(t, i, 1, 1) + bias
        here = where_ref[...] == lax.broadcasted_iota(jnp.int32, (CHUNK, IMAGES), 0) + r * CHUNK
        w = 1.0 / (1.0 + jnp.exp(jnp.where(here, logits, -logits)))
        w = jnp.where(here, -w, w).astype(bf16)
        d = dot(w, i, 1, 0)
        g = dot(w, t, 0, 0)
        if r == 0:
            dt[...] = d[:ROWS]
        t_slots[pl.ds(r * CHUNK, CHUNK), :] = d.astype(bf16)
        links.send(
            f"back{r}", t_slots.at[pl.ds(r * CHUNK + 2 * ROWS, 2 * ROWS)], t_sib.at[pl.ds(r * 2 * ROWS, 2 * ROWS)], sibling
        )
        if first:
            di[...] = g
        else:
            di[...] += g

    def from_sibling(r):
        links.arrived(f"back{r}")
        te.add(pl.ds(r * CHUNK, 2 * ROWS), (t_sib, pl.ds(r * 2 * ROWS, 2 * ROWS)))

    links.finish()
    links.arrived("sib2")
    block(2, True)
    from_sibling(2)
    te.sum_far()
    links.arrived("sib1")
    block(1, False)
    from_sibling(1)
    te.sum_far_a()
    te.sum_near(1)
    links.arrived("sib3")
    block(3, False)
    from_sibling(3)
    te.sum_near(3)
    te.sum_near_a(1)
    te.sum_near_a(3)
    links.arrived("sib0")
    block(0, False)
    i_slots[...] = di[...].astype(bf16)
    im.sum_far()
    from_sibling(0)
    te.sum_own()
    te.sum_own_b()
    im.sum_far_a()
    im.sum_near(1)
    im.sum_near(3)
    im.sum_near_a(1)
    im.sum_near_a(3)
    im.sum_own()
    own = dt[...] + t_sib[pl.ds(0, ROWS), :].astype(f32)
    text_grad[...] = norm_back(texts[...], factor * te.total(own))
    im.sum_own_b()
    image_grad[...] = norm_back(images[...], factor * im.total(di[pl.ds(0, ROWS), :]))
    links.finish()


def per_device(images, texts, match, logit_scale, logit_bias):
    spread = jnp.eye(8, dtype=jnp.int32)[:, :, None] * match[None, None, :]
    vmem = pl.BlockSpec(memory_space=pltpu.VMEM)
    smem = pl.BlockSpec(memory_space=pltpu.SMEM)
    rows = lambda n: pltpu.VMEM((n, WIDTH), bf16)
    return pl.pallas_call(
        kernel,
        out_shape=(jax.ShapeDtypeStruct((ROWS, WIDTH), f32), jax.ShapeDtypeStruct((ROWS, WIDTH), f32)),
        in_specs=[vmem, vmem, vmem, smem, smem],
        out_specs=(vmem, vmem),
        scratch_shapes=[
            rows(IMAGES), rows(TEXTS), pltpu.VMEM((8, 1, IMAGES), jnp.int32), pltpu.VMEM((1, IMAGES), jnp.int32),
            pltpu.VMEM((IMAGES, WIDTH), f32), pltpu.VMEM((ROWS, WIDTH), f32), rows(IMAGES),
            rows(4 * CUT + ROWS - CUT), rows(4 * CUT + ROWS - CUT),
            rows(2 * ROWS - CUT), rows(2 * ROWS - CUT), rows(4 * ROWS), rows(4 * ROWS),
            pltpu.SemaphoreType.DMA((SEMS,)), pltpu.SemaphoreType.DMA((SEMS,)),
        ],
        compiler_params=pltpu.CompilerParams(collective_id=0, has_side_effects=True, vmem_limit_bytes=62 << 20),
        cost_estimate=pl.CostEstimate(
            flops=6 * IMAGES * TEXTS * WIDTH, bytes_accessed=8 * ROWS * WIDTH, transcendentals=2 * IMAGES * TEXTS
        ),
        name="contrastive",
    )(images, texts, spread.reshape(8, 1, IMAGES), logit_scale, logit_bias)


def solution(mesh):
    rows = P(("blk", "group"), None)
    return jax.shard_map(
        per_device,
        mesh=mesh,
        in_specs=(rows, rows, P(("blk", "group")), P(), P()),
        out_specs=(rows, rows),
        check_vma=False,
    )
```

```python
import jax
import jax.numpy as jnp
from jax import lax
from jax.experimental import pallas as pl
from jax.experimental.pallas import tpu as pltpu
from jax.sharding import PartitionSpec as P

epsilon = 1e-06
MESH = pl.DeviceIdType.MESH
ROWS, WIDTH = 176, 1152
EARLY, LATE = 96, 80
IMAGES, TEXTS = 8 * ROWS, 16 * ROWS
SEMS = 164
bf16, f32 = jnp.bfloat16, jnp.float32


def place():
    b, g = lax.axis_index("blk"), lax.axis_index("group")
    x = lax.rem(b // 2, 2) * 2 + lax.rem(g, 2)
    return x, g // 2, b // 4, lax.rem(b, 2)


def device(x, y, z, core):
    return ((z * 2 + x // 2) * 2 + core, y * 2 + lax.rem(x, 2))


def unit_rows(x):
    values = x.astype(f32)
    scale = lax.rsqrt(jnp.sum(values * values, axis=1, keepdims=True) + epsilon)
    return values * scale, scale


def norm_back(x, grad):
    unit, scale = unit_rows(x)
    inner = jnp.sum(unit * grad, axis=1, keepdims=True)
    return scale * (grad - unit * inner)


class Links:
    def __init__(self, send_sems, recv_sems):
        self.send_sems, self.recv_sems = send_sems, recv_sems
        self.copies, self.sent = {}, 0

    def send(self, name, src, dst, target):
        k = len(self.copies)
        copy = pltpu.make_async_remote_copy(
            src_ref=src, dst_ref=dst, send_sem=self.send_sems.at[k], recv_sem=self.recv_sems.at[k],
            device_id=target, device_id_type=MESH,
        )
        copy.start()
        self.copies[name] = copy

    def arrived(self, *names):
        for name in names:
            self.copies[name].wait_recv()

    def finish(self):
        for copy in list(self.copies.values())[self.sent :]:
            copy.wait_send()
        self.sent = len(self.copies)


class Part:
    def __init__(self, tag, links, ways, slots, sums, base, stride, rows, cut, half_a, half_b, inbox, box):
        self.tag, self.links = tag, links
        self.up, self.down, self.partner = ways
        self.slots, self.sums, self.base, self.stride, self.rows = slots, sums, base, stride, rows
        self.all, self.a, self.b = (0, rows), (0, cut), (cut, rows)
        self.a0, self.a1, self.b0, self.b1 = (0, half_a), (half_a, cut), (cut, half_b), (half_b, rows)
        self.inbox, self.box, self.boxes = inbox, box, {}

    def span(self, r, p, part):
        return pl.ds(self.base + (r * self.stride + p) * self.rows + part[0], part[1] - part[0])

    def at(self, r, p, part):
        return self.slots.at[self.span(r, p, part)]

    def send(self, name, src, dst, target):
        self.links.send(self.tag + name, src, dst, target)

    def arrived(self, *names):
        self.links.arrived(*(self.tag + n for n in names))

    def gather_start(self):
        at, a, b = self.at, self.a, self.b
        self.send("gB", at(0, 0, b), at(0, 1, b), self.partner)
        self.send("gA3", at(0, 0, a), at(3, 0, a), self.up)
        self.send("gA1", at(0, 0, a), at(1, 0, a), self.down)
        self.send("gB3", at(0, 0, b), at(3, 0, b), self.up)
        self.send("gB1", at(0, 0, b), at(1, 0, b), self.down)
        self.send("gA", at(0, 0, a), at(0, 1, a), self.partner)

    def gather_pair(self):
        at, b = self.at, self.b
        self.arrived("gB")
        self.send("gC3", at(0, 1, b), at(3, 1, b), self.up)
        self.send("gC1", at(0, 1, b), at(1, 1, b), self.down)

    def gather_a(self):
        at, a = self.at, self.a
        self.arrived("gA1", "gA3")
        self.send("gA20", at(1, 0, self.a0), at(2, 0, self.a0), self.down)
        self.send("gA21", at(3, 0, self.a1), at(2, 0, self.a1), self.up)
        self.send("gD1", at(1, 0, a), at(1, 1, a), self.partner)
        self.send("gD3", at(3, 0, a), at(3, 1, a), self.partner)

    def gather_b(self):
        at = self.at
        self.arrived("gB1", "gB3")
        self.send("gB20", at(1, 0, self.b0), at(2, 0, self.b0), self.down)
        self.send("gB21", at(3, 0, self.b1), at(2, 0, self.b1), self.up)

    def gather_a2(self):
        self.arrived("gA20", "gA21")
        self.send("gD2", self.at(2, 0, self.a), self.at(2, 1, self.a), self.partner)

    def gather_c(self):
        at = self.at
        self.arrived("gC1", "gC3")
        self.send("gC20", at(1, 1, self.b0), at(2, 1, self.b0), self.down)
        self.send("gC21", at(3, 1, self.b1), at(2, 1, self.b1), self.up)

    def give(self, name, r, p, part, target):
        size = part[1] - part[0]
        where = self.boxes[name] = pl.ds(self.box, size)
        self.box += size
        self.send(name, self.sums.at[self.span(r, p, part)], self.inbox.at[where], target)

    def got(self, name):
        self.arrived(name)
        return self.inbox[self.boxes[name], :].astype(f32)

    def add(self, r, p, part, *names):
        where = self.span(r, p, part)
        total = self.sums[where, :].astype(f32)
        for name in names:
            total = total + self.got(name)
        self.sums[where, :] = total.astype(bf16)

    def sum_far(self):
        self.give("sX2", 2, 1, self.a, self.partner)
        for p in (0, 1):
            self.give(f"sH1{p}", 2, p, self.b0, self.up)
            self.give(f"sH3{p}", 2, p, self.b1, self.down)

    def sum_far_a(self):
        self.add(2, 0, self.a, "sX2")
        self.give("sHA1", 2, 0, self.a0, self.up)
        self.give("sHA3", 2, 0, self.a1, self.down)

    def sum_pair(self, r):
        self.give(f"sX{r}", r, 1, self.a, self.partner)

    def sum_near(self, r):
        half, target = (self.b0, self.up) if r == 1 else (self.b1, self.down)
        for p in (1, 0):
            self.add(r, p, half, f"sH{r}{p}")
            self.give(f"sR{r}{p}", r, p, self.b, target)

    def sum_near_a(self, r):
        half, target = (self.a0, self.up) if r == 1 else (self.a1, self.down)
        self.add(r, 0, self.a, f"sX{r}")
        self.add(r, 0, half, f"sHA{r}")
        self.give(f"sRA{r}", r, 0, self.a, target)

    def sum_own_b(self):
        self.add(0, 1, self.b, "sR11", "sR31")
        self.give("sXB", 0, 1, self.b, self.partner)

    def total(self, own):
        top = self.got("sX0") + self.got("sRA1") + self.got("sRA3")
        bottom = self.got("sR10") + self.got("sR30") + self.got("sXB")
        return own + jnp.concatenate([top, bottom], axis=0)


def dot(a, b, ca, cb):
    return lax.dot_general(a, b, (((ca,), (cb,)), ((), ())), preferred_element_type=f32)


def kernel(
    images, texts, matches, scale_ref, bias_ref, image_grad, text_grad,
    i_slots, t_slots, m_slots, where_ref, w_ref, di, dt, t_own, t_sib, i_sums, i_inbox, t_inbox, send_sems, recv_sems,
):
    x, y, z, core = place()
    odd = lax.rem(x, 2)
    xi = x + 1 - 2 * odd
    xt = lax.rem(x + 3 + 2 * odd, 4)
    y_up, y_down, y_far = lax.rem(y + 1, 4), lax.rem(y + 3, 4), lax.rem(y + 2, 4)
    z_up, z_down = lax.rem(z + 1, 4), lax.rem(z + 3, 4)
    sibling = device(x, y, z, 1 - core)
    peers = {(r, p): device((x, xi)[p], (y, y_up, y_far, y_down)[r], z, core) for r in range(4) for p in range(2)}
    t_ways = device(x, y, z_up, core), device(x, y, z_down, core), device(xt, y, z, core)
    i_ways = peers[1, 0], peers[3, 0], peers[0, 1]

    barrier = pltpu.get_barrier_semaphore()
    greeted = [d for k, d in peers.items() if k != (0, 0)] + [*t_ways, sibling]
    for d in greeted:
        pl.semaphore_signal(barrier, inc=1, device_id=d, device_id_type=MESH)
    for source, slots, late in ((images, i_slots, 8 * EARLY), (texts, t_slots, 16 * EARLY)):
        unit = unit_rows(source[...])[0].astype(bf16)
        slots[pl.ds(0, EARLY), :] = unit[:EARLY]
        slots[pl.ds(late, LATE), :] = unit[EARLY:]
    m_slots[0] = matches[0]
    pl.semaphore_wait(barrier, len(greeted))

    links = Links(send_sems, recv_sems)
    Y = Part("Y", links, i_ways, i_slots, i_sums, 0, 2, EARLY, 48, 32, 64, i_inbox, 0)
    X = Part("X", links, i_ways, i_slots, i_sums, 8 * EARLY, 2, LATE, 32, 16, 64, i_inbox, 8 * EARLY)
    U = Part("U", links, t_ways, t_slots, t_slots, 0, 4, EARLY, 48, 32, 64, t_inbox, 0)
    V = Part("V", links, t_ways, t_slots, t_slots, 16 * EARLY, 4, LATE, 32, 16, 64, t_inbox, 8 * EARLY)

    def crossing(part, r):
        return part.span(r, 2, (0, 2 * part.rows))

    def to_sibling(part, *rs):
        for r in rs:
            src = t_slots.at[part.span(r, 0, (0, 2 * part.rows))]
            links.send(f"{part.tag}to{r}", src, t_slots.at[crossing(part, r)], sibling)

    def crossed(part, *rs):
        links.arrived(*(f"{part.tag}to{r}" for r in rs))

    def sib_rows(part, r):
        return pl.ds((0 if part is U else 8 * EARLY) + r * 2 * part.rows, 2 * part.rows)

    def back_to_sibling(part, *rs):
        for r in rs:
            links.send(f"{part.tag}back{r}", t_slots.at[crossing(part, r)], t_sib.at[sib_rows(part, r)], sibling)

    def from_sibling(part, *rs):
        for r in rs:
            links.arrived(f"{part.tag}back{r}")
            mine = dt[pl.ds(r * 4 * part.rows, 2 * part.rows), :] + t_sib[sib_rows(part, r), :].astype(f32)
            if r == 0:
                t_own[pl.ds(0 if part is U else EARLY, part.rows), :] = mine[: part.rows]
            t_slots[part.span(r, 0, (0, 2 * part.rows)), :] = mine.astype(bf16)

    factor, bias = scale_ref[0], bias_ref[0]

    def nothing():
        pass

    def block(text_part, half, image_part, first_t, first_i, last_t, hooks=()):
        after_logits, between, after = (*hooks, nothing, nothing, nothing)[:3]
        tn, n = 8 * text_part.rows, 8 * image_part.rows
        t0 = text_part.base + half * tn
        t_at, i_at = pl.ds(t0, tn), pl.ds(image_part.base, n)
        logits = factor * dot(t_slots[t_at, :], i_slots[i_at, :], 1, 1) + bias
        here = where_ref[:, i_at] == lax.broadcasted_iota(jnp.int32, (tn, n), 0) + t0
        w = 1.0 / (1.0 + jnp.exp(jnp.where(here, logits, -logits)))
        w_ref[pl.ds(0, tn), pl.ds(0, n)] = jnp.where(here, -w, w).astype(bf16)
        after_logits()
        w = w_ref[pl.ds(0, tn), pl.ds(0, n)]
        g = dot(w, t_slots[t_at, :], 0, 0)
        if first_i:
            di[i_at, :] = g
        else:
            di[i_at, :] += g
        between()
        w = w_ref[pl.ds(0, tn), pl.ds(0, n)]
        d = dot(w, i_slots[i_at, :], 1, 0)
        rows = pl.ds(half * tn, tn)
        if first_t:
            dt[rows, :] = d
        else:
            dt[rows, :] += d
        if last_t:
            for r in (2 * half, 2 * half + 1):
                theirs = dt[pl.ds((r * 4 + 2) * text_part.rows, 2 * text_part.rows), :]
                t_slots[crossing(text_part, r), :] = theirs.astype(bf16)
            back_to_sibling(text_part, 2 * half, 2 * half + 1)
        after()

    def ready(part, *rs):
        for r in rs:
            where = part.span(r, 0, (0, 2 * part.rows))
            i_sums[where, :] = di[where, :].astype(bf16)

    def each(name, *parts):
        for part in parts:
            getattr(part, name)()

    def steps(*calls):
        def run():
            for call, *args in calls:
                call(*args)

        return run

    each("gather_start", Y, U)
    for r in range(4):
        for p in range(2):
            if (r, p) != (0, 0):
                k = ((4 - r) % 4) * 2 + p
                links.send(f"m{k}", matches.at[k], m_slots.at[k], peers[r, p])
    each("gather_pair", Y, U)
    each("gather_a", Y, U)
    each("gather_b", Y, U)
    U.arrived("gA")
    to_sibling(U, 0)
    each("gather_a2", Y, U)
    each("gather_c", Y, U)
    each("gather_start", X, V)

    links.arrived(*(f"m{k}" for k in range(1, 8)))
    match = m_slots[0]
    for k in range(1, 8):
        match = match + m_slots[k]
    owner = ((match.astype(f32) + 0.5) * (1.0 / ROWS)).astype(jnp.int32)
    row = match - owner * ROWS
    b, g = owner >> 3, owner & 7
    ox = ((b >> 1) & 1) * 2 + (g & 1)
    held = ((g >> 1) == y) & ((ox == x) | (ox == xt))
    slot = (((b >> 2) - z + 4) & 3) * 4 + jnp.where((b & 1) == core, 0, 2) + jnp.where(ox == x, 0, 1)
    spot = jnp.where(row < EARLY, slot * EARLY + row, 16 * EARLY + slot * LATE + row - EARLY)
    where_ref[...] = jnp.where(held, spot, -1)

    U.arrived("gD1", "gD3")
    to_sibling(U, 1, 3)
    for part in (U, Y):
        part.arrived("gB20", "gB21", "gC20", "gC21", "gD2")
    to_sibling(U, 2)
    Y.arrived("gA", "gD1", "gD3")

    crossed(U, 0, 1)
    block(U, 0, Y, True, True, False, (
        steps((each, "gather_pair", X, V)),
        steps((each, "gather_a", X, V)),
        steps((each, "gather_b", X, V), (V.arrived, "gA"), (to_sibling, V, 0)),
    ))
    crossed(U, 2, 3)
    block(U, 1, Y, True, False, False, (
        steps((each, "gather_a2", X, V)),
        steps((each, "gather_c", X, V), (V.arrived, "gD1", "gD3"), (to_sibling, V, 1, 3)),
    ))
    for part in (X, V):
        part.arrived("gB20", "gB21", "gC20", "gC21", "gD2")
    to_sibling(V, 2)
    X.arrived("gA", "gD1", "gD3")
    links.finish()

    block(U, 1, X, False, True, True)
    block(U, 0, X, False, False, True, (
        steps((from_sibling, U, 2), (U.sum_far,)),
        steps((from_sibling, U, 3), (U.sum_pair, 3)),
        steps((U.sum_far_a,)),
    ))
    crossed(V, 2, 3)
    block(V, 1, Y, True, False, False, (
        steps((from_sibling, U, 1, 0), (U.sum_pair, 1), (U.sum_near, 1), (U.sum_near, 3), (U.sum_pair, 0)),
        steps((U.sum_near_a, 1), (U.sum_near_a, 3)),
    ))
    crossed(V, 0, 1)
    block(V, 0, Y, True, False, False, (
        nothing,
        steps((U.sum_own_b,), (ready, Y, 2), (Y.sum_far,), (ready, Y, 1, 3, 0), (Y.sum_pair, 1), (Y.sum_pair, 3)),
    ))

    def finish_texts(part, rows):
        total = part.total(t_own[rows, :])
        text_grad[rows, :] = norm_back(texts[rows, :], factor * total)

    def finish_images(part, rows):
        total = part.total(di[pl.ds(part.base, part.rows), :])
        image_grad[rows, :] = norm_back(images[rows, :], factor * total)

    early, late = pl.ds(0, EARLY), pl.ds(EARLY, LATE)
    block(V, 1, X, False, False, True, (
        steps((Y.sum_far_a,), (Y.sum_pair, 0)),
        steps((Y.sum_near, 1), (Y.sum_near, 3)),
        steps((Y.sum_near_a, 1), (Y.sum_near_a, 3)),
    ))
    block(V, 0, X, False, False, True, (
        steps((from_sibling, V, 2), (V.sum_far,)),
        steps((from_sibling, V, 3), (V.sum_pair, 3), (Y.sum_own_b,), (ready, X, 2), (X.sum_far,), (ready, X, 1, 3, 0)),
        steps((X.sum_pair, 1), (X.sum_pair, 3), (V.sum_far_a,)),
    ))
    X.sum_far_a()
    X.sum_near(1)
    X.sum_near(3)
    from_sibling(V, 1)
    V.sum_pair(1)
    V.sum_near(1)
    V.sum_near(3)
    X.sum_near_a(1)
    X.sum_near_a(3)
    X.sum_pair(0)
    V.sum_near_a(1)
    V.sum_near_a(3)
    from_sibling(V, 0)
    V.sum_pair(0)
    X.sum_own_b()
    V.sum_own_b()
    finish_texts(U, early)
    finish_images(Y, early)
    finish_images(X, late)
    finish_texts(V, late)
    links.finish()


def per_device(images, texts, match, logit_scale, logit_bias):
    eye = jnp.eye(8, dtype=jnp.int32)[:, :, None]
    spread = jnp.concatenate(
        [(eye * match[:EARLY]).reshape(8, 1, 8 * EARLY), (eye * match[EARLY:]).reshape(8, 1, 8 * LATE)], axis=2
    )
    vmem = pl.BlockSpec(memory_space=pltpu.VMEM)
    smem = pl.BlockSpec(memory_space=pltpu.SMEM)
    rows = lambda n: pltpu.VMEM((n, WIDTH), bf16)
    return pl.pallas_call(
        kernel,
        out_shape=(jax.ShapeDtypeStruct((ROWS, WIDTH), f32), jax.ShapeDtypeStruct((ROWS, WIDTH), f32)),
        in_specs=[vmem, vmem, vmem, smem, smem],
        out_specs=(vmem, vmem),
        scratch_shapes=[
            rows(IMAGES), rows(TEXTS), pltpu.VMEM((8, 1, IMAGES), jnp.int32), pltpu.VMEM((1, IMAGES), jnp.int32),
            pltpu.VMEM((8 * EARLY, 8 * EARLY), bf16), pltpu.VMEM((IMAGES, WIDTH), f32), pltpu.VMEM((16 * EARLY, WIDTH), f32),
            pltpu.VMEM((ROWS, WIDTH), f32), rows(IMAGES), rows(IMAGES), rows(IMAGES), rows(IMAGES),
            pltpu.SemaphoreType.DMA((SEMS,)), pltpu.SemaphoreType.DMA((SEMS,)),
        ],
        compiler_params=pltpu.CompilerParams(collective_id=0, has_side_effects=True, vmem_limit_bytes=62 << 20),
        cost_estimate=pl.CostEstimate(
            flops=6 * IMAGES * TEXTS * WIDTH, bytes_accessed=8 * ROWS * WIDTH, transcendentals=2 * IMAGES * TEXTS
        ),
        name="contrastive",
    )(images, texts, spread, logit_scale, logit_bias)


def solution(mesh):
    rows = P(("blk", "group"), None)
    return jax.shard_map(
        per_device,
        mesh=mesh,
        in_specs=(rows, rows, P(("blk", "group")), P(), P()),
        out_specs=(rows, rows),
        check_vma=False,
    )
```

```python
import jax
import jax.numpy as jnp
from jax import lax
from jax.experimental import pallas as pl
from jax.experimental.pallas import tpu as pltpu
from jax.sharding import PartitionSpec as P

epsilon = 1e-06
MESH = pl.DeviceIdType.MESH
ROWS, WIDTH = 176, 1152
EARLY, LATE = 96, 80
FIRST, LAST = 64, 48
IMAGES, TEXTS = 8 * ROWS, 16 * ROWS
SEMS = 208
bf16, f32 = jnp.bfloat16, jnp.float32


def place():
    b, g = lax.axis_index("blk"), lax.axis_index("group")
    x = lax.rem(b // 2, 2) * 2 + lax.rem(g, 2)
    return x, g // 2, b // 4, lax.rem(b, 2)


def device(x, y, z, core):
    return ((z * 2 + x // 2) * 2 + core, y * 2 + lax.rem(x, 2))


def unit_rows(x):
    values = x.astype(f32)
    scale = lax.rsqrt(jnp.sum(values * values, axis=1, keepdims=True) + epsilon)
    return values * scale, scale


def norm_back(x, grad):
    unit, scale = unit_rows(x)
    inner = jnp.sum(unit * grad, axis=1, keepdims=True)
    return scale * (grad - unit * inner)


class Links:
    def __init__(self, send_sems, recv_sems):
        self.send_sems, self.recv_sems = send_sems, recv_sems
        self.copies, self.started, self.sent = {}, [], 0

    def plan(self, name, src, dst, target):
        self.copies[name] = len(self.copies), src, dst, target

    def copy(self, name):
        k, src, dst, target = self.copies[name]
        return pltpu.make_async_remote_copy(
            src_ref=src(), dst_ref=dst(), send_sem=self.send_sems.at[k], recv_sem=self.recv_sems.at[k],
            device_id=target, device_id_type=MESH,
        )

    def start(self, name):
        self.copy(name).start()
        self.started.append(name)

    def send(self, name, src, dst, target):
        self.plan(name, src, dst, target)
        self.start(name)

    def arrived(self, *names):
        for name in names:
            self.copy(name).wait_recv()

    def finish(self):
        for name in self.started[self.sent :]:
            self.copy(name).wait_send()
        self.sent = len(self.started)


class Part:
    def __init__(self, tag, links, ways, slots, sums, base, first, rows, cut, half_a, half_b, inbox, box):
        self.tag, self.links = tag, links
        self.up, self.down, self.partner = ways
        self.slots, self.sums, self.base, self.first, self.rows = slots, sums, base, first, rows
        self.all, self.a, self.b = (0, rows), (0, cut), (cut, rows)
        self.a0, self.a1, self.b0, self.b1 = (0, half_a), (half_a, cut), (cut, half_b), (half_b, rows)
        self.inbox, self.box, self.boxes, self.empty = inbox, box, {}, set()

    def span(self, r, p, part):
        return pl.ds(self.base + (r * 2 + p) * self.rows + part[0], part[1] - part[0])

    def at(self, r, p, part):
        return lambda: self.slots.at[self.span(r, p, part)]

    def plan(self, name, part, src, dst, target):
        if part[1] > part[0]:
            self.links.plan(self.tag + name, src, dst, target)
        else:
            self.empty.add(name)

    def give(self, *names):
        for name in names:
            if name not in self.empty:
                self.links.start(self.tag + name)

    def arrived(self, *names):
        self.links.arrived(*(self.tag + n for n in names if n not in self.empty))

    def plan_gather(self):
        up, down, partner, a, b = self.up, self.down, self.partner, self.a, self.b
        moves = [("gB", 0, 0, 0, 1, b, partner), ("gA", 0, 0, 0, 1, a, partner)]
        moves += [(f"gD{r}", r, 0, r, 1, a, partner) for r in (1, 2, 3)]
        for name, p, part in (("gA", 0, a), ("gB", 0, b), ("gC", 1, b)):
            moves += [(name + "3", 0, p, 3, p, part, up), (name + "1", 0, p, 1, p, part, down)]
            half0, half1 = (self.a0, self.a1) if part is a else (self.b0, self.b1)
            moves += [(name + "20", 1, p, 2, p, half0, down), (name + "21", 3, p, 2, p, half1, up)]
        for name, r, p, to_r, to_p, part, target in moves:
            self.plan(name, part, self.at(r, p, part), self.at(to_r, to_p, part), target)

    def gather_start(self):
        self.give("gB", "gA3", "gA1", "gB3", "gB1", "gA")

    def gather_pair(self):
        self.arrived("gB")
        self.give("gC3", "gC1")

    def gather_a(self):
        self.arrived("gA1", "gA3")
        self.give("gA20", "gA21", "gD1", "gD3")

    def gather_b(self):
        self.arrived("gB1", "gB3")
        self.give("gB20", "gB21")

    def gather_a2(self):
        self.arrived("gA20", "gA21")
        self.give("gD2")

    def gather_c(self):
        self.arrived("gC1", "gC3")
        self.give("gC20", "gC21")

    def plan_sums(self):
        up, down = self.up, self.down
        moves = [(f"sX{r}", r, 1, self.a, self.partner) for r in range(4)] + [("sXB", 0, 1, self.b, self.partner)]
        moves += [("sHA1", 2, 0, self.a0, up), ("sHA3", 2, 0, self.a1, down)]
        moves += [("sRA1", 1, 0, self.a, up), ("sRA3", 3, 0, self.a, down)]
        for p in (0, 1):
            moves += [(f"sH1{p}", 2, p, self.b0, up), (f"sH3{p}", 2, p, self.b1, down)]
            moves += [(f"sR1{p}", 1, p, self.b, up), (f"sR3{p}", 3, p, self.b, down)]
        for name, r, p, part, target in moves:
            src, size = self.span(r, p, part), part[1] - part[0]
            dst = self.boxes[name] = pl.ds(self.box, size)
            self.box += size
            self.plan(name, part, lambda src=src: self.sums.at[src], lambda dst=dst: self.inbox.at[dst], target)

    def got(self, name):
        self.arrived(name)
        return self.inbox[self.boxes[name], :].astype(f32)

    def add(self, r, p, part, *names):
        if part[1] == part[0]:
            return
        where = self.span(r, p, part)
        total = self.sums[where, :].astype(f32)
        for name in names:
            total = total + self.got(name)
        self.sums[where, :] = total.astype(bf16)

    def sum_far(self):
        self.give("sX2", "sH11", "sH31", "sH10", "sH30")

    def sum_far_a(self):
        self.add(2, 0, self.a, "sX2")
        self.give("sHA1", "sHA3")

    def sum_pair(self, r):
        self.give(f"sX{r}")

    def sum_near(self, r):
        half = self.b0 if r == 1 else self.b1
        for p in (1, 0):
            self.add(r, p, half, f"sH{r}{p}")
            self.give(f"sR{r}{p}")

    def sum_near_a(self, r):
        half = self.a0 if r == 1 else self.a1
        self.add(r, 0, self.a, f"sX{r}")
        self.add(r, 0, half, f"sHA{r}")
        self.give(f"sRA{r}")

    def sum_own_b(self):
        self.add(0, 1, self.b, "sR11", "sR31")
        self.give("sXB")

    def total(self, own):
        top = self.got("sX0") + self.got("sRA1") + self.got("sRA3")
        bottom = self.got("sR10") + self.got("sR30") + self.got("sXB")
        return own + jnp.concatenate([top, bottom], axis=0)


def floor_div(a, n):
    return ((a.astype(f32) + 0.5) * (1.0 / n)).astype(jnp.int32)


def dot(a, b, ca, cb):
    return lax.dot_general(a, b, (((ca,), (cb,)), ((), ())), preferred_element_type=f32)


def kernel(
    images, texts, matches, scale_ref, bias_ref, image_grad, text_grad,
    i_slots, t_slots, m_slots, where_ref, w_ref, di, dt, t_own, t_sib, i_sums, i_inbox, t_inbox, send_sems, recv_sems,
):
    x, y, z, core = place()
    odd = lax.rem(x, 2)
    xi = x + 1 - 2 * odd
    xt = lax.rem(x + 3 + 2 * odd, 4)
    y_up, y_down, y_far = lax.rem(y + 1, 4), lax.rem(y + 3, 4), lax.rem(y + 2, 4)
    z_up, z_down = lax.rem(z + 1, 4), lax.rem(z + 3, 4)
    sibling = device(x, y, z, 1 - core)
    peers = {(r, p): device((x, xi)[p], (y, y_up, y_far, y_down)[r], z, core) for r in range(4) for p in range(2)}
    t_ways = device(x, y, z_up, core), device(x, y, z_down, core), device(xt, y, z, core)
    i_ways = peers[1, 0], peers[3, 0], peers[0, 1]

    barrier = pltpu.get_barrier_semaphore()
    greeted = [d for k, d in peers.items() if k != (0, 0)] + [*t_ways, sibling]
    for d in greeted:
        pl.semaphore_signal(barrier, inc=1, device_id=d, device_id_type=MESH)
    unit = unit_rows(images[...])[0].astype(bf16)
    i_slots[pl.ds(0, EARLY), :] = unit[:EARLY]
    i_slots[pl.ds(8 * EARLY, LATE), :] = unit[EARLY:]
    unit = unit_rows(texts[...])[0].astype(bf16)
    t_slots[pl.ds(0, FIRST), :] = unit[:FIRST]
    t_slots[pl.ds(16 * FIRST, FIRST), :] = unit[FIRST : 2 * FIRST]
    t_slots[pl.ds(32 * FIRST, LAST), :] = unit[2 * FIRST :]
    pl.semaphore_wait(barrier, len(greeted))

    links = Links(send_sems, recv_sems)
    Y = Part("Y", links, i_ways, i_slots, i_sums, 0, 0, EARLY, 48, 32, 64, i_inbox, 0)
    X = Part("X", links, i_ways, i_slots, i_sums, 8 * EARLY, EARLY, LATE, 32, 16, 64, i_inbox, 8 * EARLY)
    T = Part("T", links, t_ways, t_slots, t_slots, 0, 0, FIRST, 32, 16, 48, t_inbox, 0)
    U = Part("U", links, t_ways, t_slots, t_slots, 16 * FIRST, FIRST, FIRST, 32, 16, 48, t_inbox, 8 * FIRST)
    V = Part("V", links, t_ways, t_slots, t_slots, 32 * FIRST, 2 * FIRST, LAST, 16, 16, 32, t_inbox, 16 * FIRST)

    def pairs(part, sibs, r, n):
        return pl.ds(part.base + ((4 * sibs + r) * 2) * part.rows, 2 * n * part.rows)

    def sib_rows(part, r, n):
        return pl.ds(part.base // 2 + r * 2 * part.rows, 2 * n * part.rows)

    def to_sibling(part, *rs):
        for r in rs:
            src, dst = pairs(part, 0, r, 1), pairs(part, 1, r, 1)
            links.send(f"{part.tag}to{r}", lambda src=src: t_slots.at[src], lambda dst=dst: t_slots.at[dst], sibling)

    def crossed(part, *rs):
        links.arrived(*(f"{part.tag}to{r}" for r in rs))

    for part in (Y, X, T, U, V):
        part.plan_gather()
        part.plan_sums()
    for part in (T, U, V):
        for r in (2, 0):
            src, dst = pairs(part, 1, r, 2), sib_rows(part, r, 2)
            links.plan(f"{part.tag}back{r}", lambda src=src: t_slots.at[src], lambda dst=dst: t_sib.at[dst], sibling)

    def back_to_sibling(part):
        for r in (2, 0):
            links.start(f"{part.tag}back{r}")

    def from_sibling(part, r):
        links.arrived(f"{part.tag}back{r}")
        mine = dt[pairs(part, 0, r, 2), :] + t_sib[sib_rows(part, r, 2), :].astype(f32)
        if r == 0:
            t_own[pl.ds(part.first, part.rows), :] = mine[: part.rows]
        t_slots[pairs(part, 0, r, 2), :] = mine.astype(bf16)

    factor, bias = scale_ref[0], bias_ref[0]

    def nothing():
        pass

    def products(text_parts, image_part, first_t, first_i, hooks):
        tn, n, turns = 16 * text_parts[0].rows, 8 * image_part.rows, len(text_parts)
        i_at = pl.ds(image_part.base, n)

        def step(k):
            def at_step(calls):
                for turn in range(turns):
                    if calls[turn] is not nothing:
                        calls[turn]() if turns == 1 else pl.when(k == turn)(calls[turn])

            t0 = text_parts[0].base + k * tn
            t0 = t0 if turns == 1 else pl.multiple_of(t0, 128)
            t_at = pl.ds(t0, tn)
            logits = factor * dot(t_slots[t_at, :], i_slots[i_at, :], 1, 1) + bias
            e = jnp.exp(-logits)
            w = 1.0 / (1.0 + e)
            here = where_ref[:, i_at] - t0 == lax.broadcasted_iota(jnp.int32, (tn, n), 0)
            w_ref[pl.ds(0, tn), pl.ds(0, n)] = jnp.where(here, -e * w, w).astype(bf16)
            at_step(hooks[0])
            g = dot(w_ref[pl.ds(0, tn), pl.ds(0, n)], t_slots[t_at, :], 0, 0)
            if not first_i:
                di[i_at, :] += g
            elif turns == 1:
                di[i_at, :] = g
            else:
                di[i_at, :] = jnp.where(k == 0, g, di[i_at, :] + g)
            at_step(hooks[1])
            d = dot(w_ref[pl.ds(0, tn), pl.ds(0, n)], i_slots[i_at, :], 1, 0)
            if first_t:
                dt[t_at, :] = d
            else:
                d = dt[t_at, :] + d
                dt[pl.ds(t0, tn // 2), :] = d[: tn // 2]
                theirs = t0 + tn // 2
                t_slots[pl.ds(theirs if turns == 1 else pl.multiple_of(theirs, 128), tn // 2), :] = d[tn // 2 :].astype(bf16)
            at_step(hooks[2])

        if turns == 1:
            step(0)
        else:
            pl.loop(0, turns)(step)

    def ready(part, *rs):
        for r in rs:
            where = part.span(r, 0, (0, 2 * part.rows))
            i_sums[where, :] = di[where, :].astype(bf16)

    def each(name, *parts):
        for part in parts:
            getattr(part, name)()

    def steps(*calls):
        def run():
            for call, *args in calls:
                call(*args)

        return run

    each("gather_start", Y, T)
    lane = lax.broadcasted_iota(jnp.int32, (1, IMAGES), 1)
    is_late = lane >= 8 * EARLY
    inner = jnp.where(is_late, lane - 8 * EARLY, lane)
    slot_of = jnp.where(is_late, floor_div(inner, LATE), floor_div(inner, EARLY))
    row_of = inner - slot_of * jnp.where(is_late, LATE, EARLY) + jnp.where(is_late, EARLY, 0)
    pick = (lax.broadcasted_iota(jnp.int32, (ROWS, IMAGES), 0) == row_of).astype(bf16)
    high, low = matches[...] >> 8, matches[...] & 255
    high, low = dot(high.astype(f32).astype(bf16), pick, 1, 0), dot(low.astype(f32).astype(bf16), pick, 1, 0)
    m_slots[0] = high.astype(jnp.int32) * 256 + low.astype(jnp.int32)
    for r in range(4):
        for p in range(2):
            if (r, p) != (0, 0):
                k = ((4 - r) % 4) * 2 + p
                links.send(f"m{k}", lambda: m_slots.at[0], lambda k=k: m_slots.at[k], peers[r, p])
    each("gather_pair", T, Y)
    each("gather_a", T, Y)
    each("gather_b", T, Y)
    U.gather_start()
    T.arrived("gA")
    to_sibling(T, 0)
    each("gather_a2", T, Y)
    each("gather_c", T, Y)
    X.gather_start()
    links.arrived(*(f"m{k}" for k in range(1, 8)))
    match = m_slots[0]
    for k in range(1, 8):
        match = jnp.where(slot_of == k, m_slots[k], match)
    owner = floor_div(match, ROWS)
    row = match - owner * ROWS
    b, g = owner >> 3, owner & 7
    ox = ((b >> 1) & 1) * 2 + (g & 1)
    held = ((g >> 1) == y) & ((ox == x) | (ox == xt))
    slot = jnp.where((b & 1) == core, 0, 8) + (((b >> 2) - z + 4) & 3) * 2 + jnp.where(ox == x, 0, 1)
    spot = jnp.where(row < FIRST, slot * FIRST + row, 16 * FIRST + slot * FIRST + row - FIRST)
    spot = jnp.where(row < 2 * FIRST, spot, 32 * FIRST + slot * LAST + row - 2 * FIRST)
    where_ref[...] = jnp.where(held, spot, -1)

    T.arrived("gD1", "gD3")
    to_sibling(T, 1, 3)
    each("gather_pair", U)
    T.arrived("gB20", "gB21", "gC20", "gC21", "gD2")
    to_sibling(T, 2)
    each("gather_a", U)
    each("gather_b", U)
    V.gather_start()
    Y.arrived("gB20", "gB21", "gC20", "gC21", "gD2", "gA", "gD1", "gD3")
    crossed(T, 0, 1, 3, 2)

    def finish_texts(part):
        rows = pl.ds(part.first, part.rows)
        total = part.total(t_own[rows, :])
        text_grad[rows, :] = norm_back(texts[rows, :], factor * total)

    def finish_images(part):
        rows = pl.ds(part.first, part.rows)
        total = part.total(di[pl.ds(part.base, part.rows), :])
        image_grad[rows, :] = norm_back(images[rows, :], factor * total)

    products((T, U), Y, True, True, (
        (
            steps((each, "gather_a2", U), (each, "gather_c", U), (each, "gather_pair", X)),
            steps((each, "gather_a2", X, V), (each, "gather_c", X, V)),
        ),
        (
            steps(
                (U.arrived, "gA", "gD1", "gD3"), (to_sibling, U, 0, 1, 3),
                (U.arrived, "gB20", "gB21", "gC20", "gC21", "gD2"), (to_sibling, U, 2),
                (each, "gather_a", X), (each, "gather_b", X),
                (each, "gather_pair", V), (each, "gather_a", V), (each, "gather_b", V),
            ),
            steps(
                (V.arrived, "gA", "gD1", "gD3"), (to_sibling, V, 0, 1, 3),
                (V.arrived, "gB20", "gB21", "gC20", "gC21", "gD2"), (to_sibling, V, 2),
            ),
        ),
        (steps((crossed, U, 0, 1, 3, 2)), nothing),
    ))
    crossed(V, 0, 1, 3, 2)
    links.finish()
    products((V,), Y, True, False, (
        (nothing,),
        (steps((ready, Y, 2), (Y.sum_far,), (ready, Y, 1, 3, 0), (Y.sum_pair, 1), (Y.sum_pair, 3), (Y.sum_pair, 0)),),
        (nothing,),
    ))
    X.arrived("gB20", "gB21", "gC20", "gC21", "gD2", "gA", "gD1", "gD3")
    products((T, U), X, False, True, (
        (nothing, steps((Y.sum_near_a, 1), (Y.sum_near_a, 3))),
        (
            steps((Y.sum_far_a,), (Y.sum_near, 1), (Y.sum_near, 3)),
            steps(
                (from_sibling, T, 2), (T.sum_far,), (from_sibling, T, 0), *((T.sum_pair, r) for r in (1, 3, 0)),
                (Y.sum_own_b,),
            ),
        ),
        (steps((back_to_sibling, T)), steps((back_to_sibling, U))),
    ))
    products((V,), X, False, False, (
        (steps((T.sum_far_a,), (T.sum_near, 1), (T.sum_near, 3)),),
        (steps(
            (ready, X, 2), (X.sum_far,), (ready, X, 1, 3, 0), *((X.sum_pair, r) for r in (1, 3, 0)),
            (from_sibling, U, 2), (U.sum_far,), (from_sibling, U, 0), *((U.sum_pair, r) for r in (1, 3, 0)),
            (T.sum_near_a, 1), (T.sum_near_a, 3),
        ),),
        (steps((back_to_sibling, V), (finish_images, Y)),),
    ))
    T.sum_own_b()
    X.sum_far_a()
    U.sum_far_a()
    for part in (X, U):
        part.sum_near(1)
        part.sum_near(3)
    from_sibling(V, 2)
    V.sum_far()
    from_sibling(V, 0)
    for r in (1, 3, 0):
        V.sum_pair(r)
    for part in (X, U):
        part.sum_near_a(1)
        part.sum_near_a(3)
    V.sum_far_a()
    V.sum_near(1)
    V.sum_near(3)
    finish_texts(T)
    U.sum_own_b()
    V.sum_near_a(1)
    V.sum_near_a(3)
    X.sum_own_b()
    finish_texts(U)
    V.sum_own_b()
    finish_images(X)
    finish_texts(V)
    links.finish()


def per_device(images, texts, match, logit_scale, logit_bias):
    vmem = pl.BlockSpec(memory_space=pltpu.VMEM)
    smem = pl.BlockSpec(memory_space=pltpu.SMEM)
    rows = lambda n: pltpu.VMEM((n, WIDTH), bf16)
    return pl.pallas_call(
        kernel,
        out_shape=(jax.ShapeDtypeStruct((ROWS, WIDTH), f32), jax.ShapeDtypeStruct((ROWS, WIDTH), f32)),
        in_specs=[vmem, vmem, vmem, smem, smem],
        out_specs=(vmem, vmem),
        scratch_shapes=[
            rows(IMAGES), rows(TEXTS), pltpu.VMEM((8, 1, IMAGES), jnp.int32), pltpu.VMEM((1, IMAGES), jnp.int32),
            pltpu.VMEM((16 * FIRST, 8 * EARLY), bf16), pltpu.VMEM((IMAGES, WIDTH), f32), pltpu.VMEM((TEXTS, WIDTH), f32),
            pltpu.VMEM((ROWS, WIDTH), f32), rows(IMAGES), rows(IMAGES), rows(IMAGES), rows(IMAGES),
            pltpu.SemaphoreType.DMA((SEMS,)), pltpu.SemaphoreType.DMA((SEMS,)),
        ],
        compiler_params=pltpu.CompilerParams(collective_id=0, has_side_effects=True, vmem_limit_bytes=62 << 20),
        cost_estimate=pl.CostEstimate(
            flops=6 * IMAGES * TEXTS * WIDTH, bytes_accessed=8 * ROWS * WIDTH, transcendentals=2 * IMAGES * TEXTS
        ),
        name="contrastive",
    )(images, texts, match[None, :], logit_scale, logit_bias)


def solution(mesh):
    rows = P(("blk", "group"), None)
    return jax.shard_map(
        per_device,
        mesh=mesh,
        in_specs=(rows, rows, P(("blk", "group")), P(), P()),
        out_specs=(rows, rows),
        check_vma=False,
    )
```

```python
import jax
import jax.numpy as jnp
from jax import lax
from jax.experimental import pallas as pl
from jax.experimental.pallas import tpu as pltpu
from jax.sharding import PartitionSpec as P

epsilon = 1e-06
MESH = pl.DeviceIdType.MESH
ROWS, WIDTH = 176, 1152
EARLY, LATE = 80, 96
FIRST, LAST = 64, 48
IMAGES, TEXTS = 8 * ROWS, 16 * ROWS
SEMS = 208
bf16, f32 = jnp.bfloat16, jnp.float32


def place():
    b, g = lax.axis_index("blk"), lax.axis_index("group")
    x = lax.rem(b // 2, 2) * 2 + lax.rem(g, 2)
    return x, g // 2, b // 4, lax.rem(b, 2)


def device(x, y, z, core):
    return ((z * 2 + x // 2) * 2 + core, y * 2 + lax.rem(x, 2))


def unit_rows(x):
    values = x.astype(f32)
    scale = lax.rsqrt(jnp.sum(values * values, axis=1, keepdims=True) + epsilon)
    return values * scale, scale


def norm_back(x, grad):
    unit, scale = unit_rows(x)
    inner = jnp.sum(unit * grad, axis=1, keepdims=True)
    return scale * (grad - unit * inner)


class Links:
    def __init__(self, send_sems, recv_sems):
        self.send_sems, self.recv_sems = send_sems, recv_sems
        self.copies, self.started, self.sent = {}, [], 0

    def plan(self, name, src, dst, target):
        self.copies[name] = len(self.copies), src, dst, target

    def copy(self, name):
        k, src, dst, target = self.copies[name]
        return pltpu.make_async_remote_copy(
            src_ref=src(), dst_ref=dst(), send_sem=self.send_sems.at[k], recv_sem=self.recv_sems.at[k],
            device_id=target, device_id_type=MESH,
        )

    def start(self, name):
        self.copy(name).start()
        self.started.append(name)

    def send(self, name, src, dst, target):
        self.plan(name, src, dst, target)
        self.start(name)

    def arrived(self, *names):
        for name in names:
            self.copy(name).wait_recv()

    def finish(self):
        for name in self.started[self.sent :]:
            self.copy(name).wait_send()
        self.sent = len(self.started)


class Part:
    def __init__(self, tag, links, ways, slots, sums, base, first, rows, cut, half_a, half_b, inbox, box):
        self.tag, self.links = tag, links
        self.up, self.down, self.partner = ways
        self.slots, self.sums, self.base, self.first, self.rows = slots, sums, base, first, rows
        self.all, self.a, self.b = (0, rows), (0, cut), (cut, rows)
        self.a0, self.a1 = (0, half_a), (half_a, cut)
        self.halves = tuple(((cut, at), (at, rows)) for at in (half_b, cut + rows - half_b))
        self.inbox, self.box, self.boxes, self.empty = inbox, box, {}, set()

    def span(self, r, p, part):
        return pl.ds(self.base + (r * 2 + p) * self.rows + part[0], part[1] - part[0])

    def at(self, r, p, part):
        return lambda: self.slots.at[self.span(r, p, part)]

    def plan(self, name, part, src, dst, target):
        if part[1] > part[0]:
            self.links.plan(self.tag + name, src, dst, target)
        else:
            self.empty.add(name)

    def give(self, *names):
        for name in names:
            if name not in self.empty:
                self.links.start(self.tag + name)

    def arrived(self, *names):
        self.links.arrived(*(self.tag + n for n in names if n not in self.empty))

    def plan_gather(self):
        up, down, partner, a, b = self.up, self.down, self.partner, self.a, self.b
        moves = [("gB", 0, 0, 0, 1, b, partner), ("gA", 0, 0, 0, 1, a, partner)]
        moves += [(f"gD{r}", r, 0, r, 1, a, partner) for r in (1, 2, 3)]
        for name, p, part in (("gA", 0, a), ("gB", 0, b), ("gC", 1, b)):
            moves += [(name + "3", 0, p, 3, p, part, up), (name + "1", 0, p, 1, p, part, down)]
            half0, half1 = (self.a0, self.a1) if part is a else self.halves[p]
            moves += [(name + "20", 1, p, 2, p, half0, down), (name + "21", 3, p, 2, p, half1, up)]
        for name, r, p, to_r, to_p, part, target in moves:
            self.plan(name, part, self.at(r, p, part), self.at(to_r, to_p, part), target)

    def gather_start(self):
        self.give("gB", "gA3", "gA1", "gB3", "gB1", "gA")

    def gather_pair(self):
        self.arrived("gB")
        self.give("gC3", "gC1")

    def gather_a(self):
        self.arrived("gA1", "gA3")
        self.give("gA20", "gA21", "gD1", "gD3")

    def gather_b(self):
        self.arrived("gB1", "gB3")
        self.give("gB20", "gB21")

    def gather_a2(self):
        self.arrived("gA20", "gA21")
        self.give("gD2")

    def gather_c(self):
        self.arrived("gC1", "gC3")
        self.give("gC20", "gC21")

    def plan_sums(self):
        up, down = self.up, self.down
        moves = [(f"sX{r}", r, 1, self.a, self.partner) for r in range(4)] + [("sXB", 0, 1, self.b, self.partner)]
        moves += [("sHA1", 2, 0, self.a0, up), ("sHA3", 2, 0, self.a1, down)]
        moves += [("sRA1", 1, 0, self.a, up), ("sRA3", 3, 0, self.a, down)]
        for p in (0, 1):
            moves += [(f"sH1{p}", 2, p, self.halves[p][0], up), (f"sH3{p}", 2, p, self.halves[p][1], down)]
            moves += [(f"sR1{p}", 1, p, self.b, up), (f"sR3{p}", 3, p, self.b, down)]
        for name, r, p, part, target in moves:
            src, size = self.span(r, p, part), part[1] - part[0]
            dst = self.boxes[name] = pl.ds(self.box, size)
            self.box += size
            self.plan(name, part, lambda src=src: self.sums.at[src], lambda dst=dst: self.inbox.at[dst], target)

    def got(self, name):
        self.arrived(name)
        return self.inbox[self.boxes[name], :].astype(f32)

    def add(self, r, p, part, *names):
        if part[1] == part[0]:
            return
        where = self.span(r, p, part)
        total = self.sums[where, :].astype(f32)
        for name in names:
            total = total + self.got(name)
        self.sums[where, :] = total.astype(bf16)

    def sum_far(self):
        self.give("sX2", "sH11", "sH31", "sH10", "sH30")

    def sum_far_a(self):
        self.add(2, 0, self.a, "sX2")
        self.give("sHA1", "sHA3")

    def sum_pair(self, r):
        self.give(f"sX{r}")

    def sum_near(self, r):
        for p in (1, 0):
            self.add(r, p, self.halves[p][r // 2], f"sH{r}{p}")
            self.give(f"sR{r}{p}")

    def sum_near_a(self, r):
        half = self.a0 if r == 1 else self.a1
        self.add(r, 0, self.a, f"sX{r}")
        self.add(r, 0, half, f"sHA{r}")
        self.give(f"sRA{r}")

    def sum_own_b(self):
        self.add(0, 1, self.b, "sR11", "sR31")
        self.give("sXB")

    def total(self, own):
        top = self.got("sX0") + self.got("sRA1") + self.got("sRA3")
        bottom = self.got("sR10") + self.got("sR30") + self.got("sXB")
        return own + jnp.concatenate([top, bottom], axis=0)


def floor_div(a, n):
    return ((a.astype(f32) + 0.5) * (1.0 / n)).astype(jnp.int32)


def dot(a, b, ca, cb):
    return lax.dot_general(a, b, (((ca,), (cb,)), ((), ())), preferred_element_type=f32)


def kernel(
    images, texts, matches, scale_ref, bias_ref, image_grad, text_grad,
    i_slots, t_slots, m_slots, where_ref, w_ref, di, dt, t_own, t_out, t_sib, i_sums, i_inbox, t_inbox, send_sems, recv_sems,
):
    x, y, z, core = place()
    odd = lax.rem(x, 2)
    xi = x + 1 - 2 * odd
    xt = lax.rem(x + 3 + 2 * odd, 4)
    y_up, y_down, y_far = lax.rem(y + 1, 4), lax.rem(y + 3, 4), lax.rem(y + 2, 4)
    z_up, z_down = lax.rem(z + 1, 4), lax.rem(z + 3, 4)
    sibling = device(x, y, z, 1 - core)
    peers = {(r, p): device((x, xi)[p], (y, y_up, y_far, y_down)[r], z, core) for r in range(4) for p in range(2)}
    t_ways = device(x, y, z_up, core), device(x, y, z_down, core), device(xt, y, z, core)
    i_ways = peers[1, 0], peers[3, 0], peers[0, 1]

    barrier = pltpu.get_barrier_semaphore()
    greeted = [d for k, d in peers.items() if k != (0, 0)] + [*t_ways, sibling]
    for d in greeted:
        pl.semaphore_signal(barrier, inc=1, device_id=d, device_id_type=MESH)
    unit = unit_rows(images[...])[0].astype(bf16)
    i_slots[pl.ds(0, EARLY), :] = unit[:EARLY]
    i_slots[pl.ds(8 * EARLY, LATE), :] = unit[EARLY:]
    unit = unit_rows(texts[...])[0].astype(bf16)
    t_slots[pl.ds(0, FIRST), :] = unit[:FIRST]
    t_slots[pl.ds(16 * FIRST, FIRST), :] = unit[FIRST : 2 * FIRST]
    t_slots[pl.ds(32 * FIRST, LAST), :] = unit[2 * FIRST :]
    pl.semaphore_wait(barrier, len(greeted))

    links = Links(send_sems, recv_sems)
    Y = Part("Y", links, i_ways, i_slots, i_sums, 0, 0, EARLY, 32, 16, 64, i_inbox, 0)
    X = Part("X", links, i_ways, i_slots, i_sums, 8 * EARLY, EARLY, LATE, 48, 32, 64, i_inbox, 8 * EARLY)
    T = Part("T", links, t_ways, t_slots, t_slots, 0, 0, FIRST, 32, 16, 48, t_inbox, 0)
    U = Part("U", links, t_ways, t_slots, t_slots, 16 * FIRST, FIRST, FIRST, 32, 16, 48, t_inbox, 8 * FIRST)
    V = Part("V", links, t_ways, t_slots, t_slots, 32 * FIRST, 2 * FIRST, LAST, 16, 16, 32, t_inbox, 16 * FIRST)

    def pairs(part, sibs, r, n):
        return pl.ds(part.base + ((4 * sibs + r) * 2) * part.rows, 2 * n * part.rows)

    def sib_rows(part, r, n):
        return pl.ds(part.base // 2 + r * 2 * part.rows, 2 * n * part.rows)

    def to_sibling(part, *rs):
        for r in rs:
            src, dst = pairs(part, 0, r, 1), pairs(part, 1, r, 1)
            links.send(f"{part.tag}to{r}", lambda src=src: t_slots.at[src], lambda dst=dst: t_slots.at[dst], sibling)

    def crossed(part, *rs):
        links.arrived(*(f"{part.tag}to{r}" for r in rs))

    for part in (Y, X, T, U, V):
        part.plan_gather()
        part.plan_sums()
    for part in (T, U, V):
        for r in (2, 0):
            where = sib_rows(part, r, 2)
            links.plan(
                f"{part.tag}back{r}", lambda where=where: t_out.at[where], lambda where=where: t_sib.at[where], sibling
            )

    def back_to_sibling(part):
        for r in (2, 0):
            links.start(f"{part.tag}back{r}")

    def from_sibling(part, r):
        links.arrived(f"{part.tag}back{r}")
        mine = dt[pairs(part, 0, r, 2), :] + t_sib[sib_rows(part, r, 2), :].astype(f32)
        if r == 0:
            t_own[pl.ds(part.first, part.rows), :] = mine[: part.rows]
        t_slots[pairs(part, 0, r, 2), :] = mine.astype(bf16)

    factor, bias = scale_ref[0], bias_ref[0]

    def nothing():
        pass

    def products(text_parts, image_part, first_t, first_i, hooks, texts_first=False):
        tn, n, turns = 16 * text_parts[0].rows, 8 * image_part.rows, len(text_parts)
        i_at = pl.ds(image_part.base, n)

        def image_grads(k, t0):
            g = dot(w_ref[pl.ds(0, tn), pl.ds(0, n)], t_slots[pl.ds(t0, tn), :], 0, 0)
            if not first_i:
                di[i_at, :] += g
            elif turns == 1:
                di[i_at, :] = g
            else:
                di[i_at, :] = jnp.where(k == 0, g, di[i_at, :] + g)

        def text_grads(k, t0):
            d = dot(w_ref[pl.ds(0, tn), pl.ds(0, n)], i_slots[i_at, :], 1, 0)
            if first_t:
                dt[pl.ds(t0, tn), :] = d
            else:
                d = dt[pl.ds(t0, tn), :] + d
                dt[pl.ds(t0, tn // 2), :] = d[: tn // 2]
                out = t0 // 2 if turns == 1 else pl.multiple_of(text_parts[0].base // 2 + k * (tn // 2), 128)
                t_out[pl.ds(out, tn // 2), :] = d[tn // 2 :].astype(bf16)

        def step(k):
            def at_step(calls):
                for turn in range(turns):
                    if calls[turn] is not nothing:
                        calls[turn]() if turns == 1 else pl.when(k == turn)(calls[turn])

            t0 = text_parts[0].base + k * tn
            t0 = t0 if turns == 1 else pl.multiple_of(t0, 128)
            t_at = pl.ds(t0, tn)
            logits = factor * dot(t_slots[t_at, :], i_slots[i_at, :], 1, 1) + bias
            e = jnp.exp(-logits)
            w = 1.0 / (1.0 + e)
            here = where_ref[:, i_at] - t0 == lax.broadcasted_iota(jnp.int32, (tn, n), 0)
            w_ref[pl.ds(0, tn), pl.ds(0, n)] = jnp.where(here, -e * w, w).astype(bf16)
            at_step(hooks[0])
            order = (text_grads, image_grads) if texts_first else (image_grads, text_grads)
            order[0](k, t0)
            at_step(hooks[1])
            order[1](k, t0)
            at_step(hooks[2])

        if turns == 1:
            step(0)
        else:
            pl.loop(0, turns)(step)

    def ready(part, *rs):
        for r in rs:
            where = part.span(r, 0, (0, 2 * part.rows))
            i_sums[where, :] = di[where, :].astype(bf16)

    def each(name, *parts):
        for part in parts:
            getattr(part, name)()

    def steps(*calls):
        def run():
            for call, *args in calls:
                call(*args)

        return run

    each("gather_start", Y, T)
    lane = lax.broadcasted_iota(jnp.int32, (1, IMAGES), 1)
    is_late = lane >= 8 * EARLY
    inner = jnp.where(is_late, lane - 8 * EARLY, lane)
    slot_of = jnp.where(is_late, floor_div(inner, LATE), floor_div(inner, EARLY))
    row_of = inner - slot_of * jnp.where(is_late, LATE, EARLY) + jnp.where(is_late, EARLY, 0)
    pick = (lax.broadcasted_iota(jnp.int32, (ROWS, IMAGES), 0) == row_of).astype(bf16)
    high, low = matches[...] >> 8, matches[...] & 255
    high, low = dot(high.astype(f32).astype(bf16), pick, 1, 0), dot(low.astype(f32).astype(bf16), pick, 1, 0)
    m_slots[0] = high.astype(jnp.int32) * 256 + low.astype(jnp.int32)
    for r in range(4):
        for p in range(2):
            if (r, p) != (0, 0):
                k = ((4 - r) % 4) * 2 + p
                links.send(f"m{k}", lambda: m_slots.at[0], lambda k=k: m_slots.at[k], peers[r, p])
    each("gather_pair", T, Y)
    each("gather_a", T, Y)
    each("gather_b", T, Y)
    U.gather_start()
    T.arrived("gA")
    to_sibling(T, 0)
    each("gather_a2", T, Y)
    each("gather_c", T, Y)
    X.gather_start()
    links.arrived(*(f"m{k}" for k in range(1, 8)))
    match = m_slots[0]
    for k in range(1, 8):
        match = jnp.where(slot_of == k, m_slots[k], match)
    owner = floor_div(match, ROWS)
    row = match - owner * ROWS
    b, g = owner >> 3, owner & 7
    ox = ((b >> 1) & 1) * 2 + (g & 1)
    held = ((g >> 1) == y) & ((ox == x) | (ox == xt))
    slot = jnp.where((b & 1) == core, 0, 8) + (((b >> 2) - z + 4) & 3) * 2 + jnp.where(ox == x, 0, 1)
    spot = jnp.where(row < FIRST, slot * FIRST + row, 16 * FIRST + slot * FIRST + row - FIRST)
    spot = jnp.where(row < 2 * FIRST, spot, 32 * FIRST + slot * LAST + row - 2 * FIRST)
    where_ref[...] = jnp.where(held, spot, -1)

    T.arrived("gD1", "gD3")
    to_sibling(T, 1, 3)
    each("gather_pair", U)
    T.arrived("gB20", "gB21", "gC20", "gC21", "gD2")
    to_sibling(T, 2)
    each("gather_a", U)
    each("gather_b", U)
    V.gather_start()
    Y.arrived("gB20", "gB21", "gC20", "gC21", "gD2", "gA", "gD1", "gD3")
    crossed(T, 0, 1, 3, 2)

    def finish_texts(part):
        rows = pl.ds(part.first, part.rows)
        total = part.total(t_own[rows, :])
        text_grad[rows, :] = norm_back(texts[rows, :], factor * total)

    def finish_images(part):
        rows = pl.ds(part.first, part.rows)
        total = part.total(di[pl.ds(part.base, part.rows), :])
        image_grad[rows, :] = norm_back(images[rows, :], factor * total)

    products((T, U), Y, True, True, (
        (
            steps((each, "gather_a2", U), (each, "gather_c", U), (each, "gather_pair", X)),
            steps((each, "gather_a2", X, V), (each, "gather_c", X, V)),
        ),
        (
            steps(
                (U.arrived, "gA", "gD1", "gD3"), (to_sibling, U, 0, 1, 3),
                (U.arrived, "gB20", "gB21", "gC20", "gC21", "gD2"), (to_sibling, U, 2),
                (each, "gather_a", X), (each, "gather_b", X),
                (each, "gather_pair", V), (each, "gather_a", V), (each, "gather_b", V),
            ),
            steps(
                (V.arrived, "gA", "gD1", "gD3"), (to_sibling, V, 0, 1, 3),
                (V.arrived, "gB20", "gB21", "gC20", "gC21", "gD2"), (to_sibling, V, 2),
            ),
        ),
        (steps((crossed, U, 0, 1, 3, 2)), nothing),
    ))
    crossed(V, 0, 1, 3, 2)
    links.finish()
    products((V,), Y, True, False, (
        (nothing,),
        (steps((ready, Y, 2), (Y.sum_far,), (ready, Y, 1, 3, 0), (Y.sum_pair, 1), (Y.sum_pair, 3), (Y.sum_pair, 0)),),
        (nothing,),
    ))
    X.arrived("gB20", "gB21", "gC20", "gC21", "gD2", "gA", "gD1", "gD3")
    products((T, U), X, False, True, (
        (
            nothing,
            steps(
                (from_sibling, T, 2), (T.sum_far,), (from_sibling, T, 0), *((T.sum_pair, r) for r in (1, 3, 0)),
                (Y.sum_near_a, 1), (Y.sum_near_a, 3),
            ),
        ),
        (
            steps((back_to_sibling, T), (Y.sum_far_a,), (Y.sum_near, 1), (Y.sum_near, 3)),
            steps((back_to_sibling, U), (T.sum_far_a,), (T.sum_near, 1), (T.sum_near, 3)),
        ),
        (nothing, steps((T.sum_near_a, 1), (T.sum_near_a, 3), (Y.sum_own_b,))),
    ), texts_first=True)
    products((V,), X, False, False, (
        (steps(
            (from_sibling, U, 2), (U.sum_far,), (from_sibling, U, 0), *((U.sum_pair, r) for r in (1, 3, 0)),
        ),),
        (steps(
            (ready, X, 2), (X.sum_far,), (ready, X, 1, 3, 0), *((X.sum_pair, r) for r in (1, 3, 0)),
            (U.sum_far_a,), (U.sum_near, 1), (U.sum_near, 3),
        ),),
        (steps((back_to_sibling, V), (finish_images, Y)),),
    ))
    T.sum_own_b()
    X.sum_far_a()
    X.sum_near(1)
    X.sum_near(3)
    from_sibling(V, 2)
    V.sum_far()
    from_sibling(V, 0)
    for r in (1, 3, 0):
        V.sum_pair(r)
    for part in (X, U):
        part.sum_near_a(1)
        part.sum_near_a(3)
    V.sum_far_a()
    V.sum_near(1)
    V.sum_near(3)
    finish_texts(T)
    U.sum_own_b()
    V.sum_near_a(1)
    V.sum_near_a(3)
    X.sum_own_b()
    finish_texts(U)
    V.sum_own_b()
    finish_images(X)
    finish_texts(V)
    links.finish()


def per_device(images, texts, match, logit_scale, logit_bias):
    vmem = pl.BlockSpec(memory_space=pltpu.VMEM)
    smem = pl.BlockSpec(memory_space=pltpu.SMEM)
    rows = lambda n: pltpu.VMEM((n, WIDTH), bf16)
    return pl.pallas_call(
        kernel,
        out_shape=(pltpu.VMEM((ROWS, WIDTH), f32), pltpu.VMEM((ROWS, WIDTH), f32)),
        in_specs=[vmem, vmem, vmem, smem, smem],
        out_specs=(vmem, vmem),
        scratch_shapes=[
            rows(IMAGES), rows(TEXTS), pltpu.VMEM((8, 1, IMAGES), jnp.int32), pltpu.VMEM((1, IMAGES), jnp.int32),
            pltpu.VMEM((16 * FIRST, 8 * LATE), bf16), pltpu.VMEM((IMAGES, WIDTH), f32), pltpu.VMEM((TEXTS, WIDTH), f32),
            pltpu.VMEM((ROWS, WIDTH), f32), rows(IMAGES), rows(IMAGES), rows(IMAGES), rows(IMAGES), rows(IMAGES),
            pltpu.SemaphoreType.DMA((SEMS,)), pltpu.SemaphoreType.DMA((SEMS,)),
        ],
        compiler_params=pltpu.CompilerParams(collective_id=0, has_side_effects=True, vmem_limit_bytes=60 << 20),
        cost_estimate=pl.CostEstimate(
            flops=6 * IMAGES * TEXTS * WIDTH, bytes_accessed=8 * ROWS * WIDTH, transcendentals=2 * IMAGES * TEXTS
        ),
        name="contrastive",
    )(images, texts, match[None, :], logit_scale, logit_bias)


def solution(mesh):
    rows = P(("blk", "group"), None)
    return jax.shard_map(
        per_device,
        mesh=mesh,
        in_specs=(rows, rows, P(("blk", "group")), P(), P()),
        out_specs=(rows, rows),
        check_vma=False,
    )
```

```python
import jax
import jax.numpy as jnp
from jax import lax
from jax.experimental import pallas as pl
from jax.experimental.pallas import tpu as pltpu
from jax.sharding import PartitionSpec as P

epsilon = 1e-06
MESH = pl.DeviceIdType.MESH
ROWS, WIDTH = 176, 1152
EARLY, LATE = 80, 96
FIRST, LAST = 64, 48
IMAGES, TEXTS = 8 * ROWS, 16 * ROWS
SEMS = 208
bf16, f32 = jnp.bfloat16, jnp.float32


def place():
    b, g = lax.axis_index("blk"), lax.axis_index("group")
    x = lax.rem(b // 2, 2) * 2 + lax.rem(g, 2)
    return x, g // 2, b // 4, lax.rem(b, 2)


def device(x, y, z, core):
    return ((z * 2 + x // 2) * 2 + core, y * 2 + lax.rem(x, 2))


def unit_rows(x):
    values = x.astype(f32)
    scale = lax.rsqrt(jnp.sum(values * values, axis=1, keepdims=True) + epsilon)
    return values * scale, scale


def norm_back(x, grad):
    unit, scale = unit_rows(x)
    inner = jnp.sum(unit * grad, axis=1, keepdims=True)
    return scale * (grad - unit * inner)


class Links:
    def __init__(self, send_sems, recv_sems):
        self.send_sems, self.recv_sems = send_sems, recv_sems
        self.copies, self.started, self.sent = {}, [], 0

    def plan(self, name, src, dst, target):
        self.copies[name] = len(self.copies), src, dst, target

    def copy(self, name):
        k, src, dst, target = self.copies[name]
        return pltpu.make_async_remote_copy(
            src_ref=src(), dst_ref=dst(), send_sem=self.send_sems.at[k], recv_sem=self.recv_sems.at[k],
            device_id=target, device_id_type=MESH,
        )

    def start(self, name):
        self.copy(name).start()
        self.started.append(name)

    def send(self, name, src, dst, target):
        self.plan(name, src, dst, target)
        self.start(name)

    def arrived(self, *names):
        for name in names:
            self.copy(name).wait_recv()

    def finish(self):
        for name in self.started[self.sent :]:
            self.copy(name).wait_send()
        self.sent = len(self.started)


class Part:
    def __init__(self, tag, links, ways, slots, sums, base, first, rows, cut, half_a, half_b, inbox, box):
        self.tag, self.links = tag, links
        self.up, self.down, self.partner = ways
        self.slots, self.sums, self.base, self.first, self.rows = slots, sums, base, first, rows
        self.all, self.a, self.b = (0, rows), (0, cut), (cut, rows)
        self.a0, self.a1 = (0, half_a), (half_a, cut)
        self.halves = tuple(((cut, at), (at, rows)) for at in (half_b, cut + rows - half_b))
        self.inbox, self.box, self.boxes, self.empty = inbox, box, {}, set()

    def span(self, r, p, part):
        return pl.ds(self.base + (r * 2 + p) * self.rows + part[0], part[1] - part[0])

    def at(self, r, p, part):
        return lambda: self.slots.at[self.span(r, p, part)]

    def plan(self, name, part, src, dst, target):
        if part[1] > part[0]:
            self.links.plan(self.tag + name, src, dst, target)
        else:
            self.empty.add(name)

    def give(self, *names):
        for name in names:
            if name not in self.empty:
                self.links.start(self.tag + name)

    def arrived(self, *names):
        self.links.arrived(*(self.tag + n for n in names if n not in self.empty))

    def plan_gather(self):
        up, down, partner, a, b = self.up, self.down, self.partner, self.a, self.b
        moves = [("gB", 0, 0, 0, 1, b, partner), ("gA", 0, 0, 0, 1, a, partner)]
        moves += [(f"gD{r}", r, 0, r, 1, a, partner) for r in (1, 2, 3)]
        for name, p, part in (("gA", 0, a), ("gB", 0, b), ("gC", 1, b)):
            moves += [(name + "3", 0, p, 3, p, part, up), (name + "1", 0, p, 1, p, part, down)]
            half0, half1 = (self.a0, self.a1) if part is a else self.halves[p]
            moves += [(name + "20", 1, p, 2, p, half0, down), (name + "21", 3, p, 2, p, half1, up)]
        for name, r, p, to_r, to_p, part, target in moves:
            self.plan(name, part, self.at(r, p, part), self.at(to_r, to_p, part), target)

    def gather_start(self):
        self.give("gB", "gA3", "gA1", "gB3", "gB1", "gA")

    def gather_pair(self):
        self.arrived("gB")
        self.give("gC3", "gC1")

    def gather_a(self):
        self.arrived("gA1", "gA3")
        self.give("gA20", "gA21", "gD1", "gD3")

    def gather_b(self):
        self.arrived("gB1", "gB3")
        self.give("gB20", "gB21")

    def gather_a2(self):
        self.arrived("gA20", "gA21")
        self.give("gD2")

    def gather_c(self):
        self.arrived("gC1", "gC3")
        self.give("gC20", "gC21")

    def plan_sums(self):
        up, down = self.up, self.down
        moves = [(f"sX{r}", r, 1, self.a, self.partner) for r in range(4)] + [("sXB", 0, 1, self.b, self.partner)]
        moves += [("sHA1", 2, 0, self.a0, up), ("sHA3", 2, 0, self.a1, down)]
        moves += [("sRA1", 1, 0, self.a, up), ("sRA3", 3, 0, self.a, down)]
        for p in (0, 1):
            moves += [(f"sH1{p}", 2, p, self.halves[p][0], up), (f"sH3{p}", 2, p, self.halves[p][1], down)]
            moves += [(f"sR1{p}", 1, p, self.b, up), (f"sR3{p}", 3, p, self.b, down)]
        for name, r, p, part, target in moves:
            src, size = self.span(r, p, part), part[1] - part[0]
            dst = self.boxes[name] = pl.ds(self.box, size)
            self.box += size
            self.plan(name, part, lambda src=src: self.sums.at[src], lambda dst=dst: self.inbox.at[dst], target)

    def got(self, name):
        self.arrived(name)
        return self.inbox[self.boxes[name], :].astype(f32)

    def add(self, r, p, part, *names):
        if part[1] == part[0]:
            return
        where = self.span(r, p, part)
        total = self.sums[where, :].astype(f32)
        for name in names:
            total = total + self.got(name)
        self.sums[where, :] = total.astype(bf16)

    def sum_far(self):
        self.give("sX2", "sH11", "sH31", "sH10", "sH30")

    def sum_far_a(self):
        self.add(2, 0, self.a, "sX2")
        self.give("sHA1", "sHA3")

    def sum_pair(self, r):
        self.give(f"sX{r}")

    def sum_near(self, r):
        for p in (1, 0):
            self.add(r, p, self.halves[p][r // 2], f"sH{r}{p}")
            self.give(f"sR{r}{p}")

    def sum_near_a(self, r):
        half = self.a0 if r == 1 else self.a1
        self.add(r, 0, self.a, f"sX{r}")
        self.add(r, 0, half, f"sHA{r}")
        self.give(f"sRA{r}")

    def sum_own_b(self):
        self.add(0, 1, self.b, "sR11", "sR31")
        self.give("sXB")

    def total(self, own):
        top = self.got("sX0") + self.got("sRA1") + self.got("sRA3")
        bottom = self.got("sR10") + self.got("sR30") + self.got("sXB")
        return own + jnp.concatenate([top, bottom], axis=0)


def floor_div(a, n):
    return ((a.astype(f32) + 0.5) * (1.0 / n)).astype(jnp.int32)


def dot(a, b, ca, cb):
    return lax.dot_general(a, b, (((ca,), (cb,)), ((), ())), preferred_element_type=f32)


def kernel(
    images, texts, matches, scale_ref, bias_ref, image_grad, text_grad,
    i_slots, t_slots, m_slots, where_ref, w_ref, di, dt, t_own, t_out, t_sib, i_sums, i_inbox, t_inbox, send_sems, recv_sems,
):
    x, y, z, core = place()
    odd = lax.rem(x, 2)
    xi = x + 1 - 2 * odd
    xt = lax.rem(x + 3 + 2 * odd, 4)
    y_up, y_down, y_far = lax.rem(y + 1, 4), lax.rem(y + 3, 4), lax.rem(y + 2, 4)
    z_up, z_down = lax.rem(z + 1, 4), lax.rem(z + 3, 4)
    sibling = device(x, y, z, 1 - core)
    peers = {(r, p): device((x, xi)[p], (y, y_up, y_far, y_down)[r], z, core) for r in range(4) for p in range(2)}
    t_ways = device(x, y, z_up, core), device(x, y, z_down, core), device(xt, y, z, core)
    i_ways = peers[1, 0], peers[3, 0], peers[0, 1]

    barrier = pltpu.get_barrier_semaphore()
    greeted = [d for k, d in peers.items() if k != (0, 0)] + [*t_ways, sibling]
    for d in greeted:
        pl.semaphore_signal(barrier, inc=1, device_id=d, device_id_type=MESH)
    unit = unit_rows(images[...])[0].astype(bf16)
    i_slots[pl.ds(0, EARLY), :] = unit[:EARLY]
    i_slots[pl.ds(8 * EARLY, LATE), :] = unit[EARLY:]
    unit = unit_rows(texts[...])[0].astype(bf16)
    t_slots[pl.ds(0, FIRST), :] = unit[:FIRST]
    t_slots[pl.ds(16 * FIRST, FIRST), :] = unit[FIRST : 2 * FIRST]
    t_slots[pl.ds(32 * FIRST, LAST), :] = unit[2 * FIRST :]
    pl.semaphore_wait(barrier, len(greeted))

    links = Links(send_sems, recv_sems)
    Y = Part("Y", links, i_ways, i_slots, i_sums, 0, 0, EARLY, 32, 16, 64, i_inbox, 0)
    X = Part("X", links, i_ways, i_slots, i_sums, 8 * EARLY, EARLY, LATE, 48, 32, 64, i_inbox, 8 * EARLY)
    T = Part("T", links, t_ways, t_slots, t_slots, 0, 0, FIRST, 32, 16, 48, t_inbox, 0)
    U = Part("U", links, t_ways, t_slots, t_slots, 16 * FIRST, FIRST, FIRST, 32, 16, 48, t_inbox, 8 * FIRST)
    V = Part("V", links, t_ways, t_slots, t_slots, 32 * FIRST, 2 * FIRST, LAST, 16, 16, 32, t_inbox, 16 * FIRST)

    def pairs(part, sibs, r, n):
        return pl.ds(part.base + ((4 * sibs + r) * 2) * part.rows, 2 * n * part.rows)

    def sib_rows(part, r, n):
        return pl.ds(part.base // 2 + r * 2 * part.rows, 2 * n * part.rows)

    def to_sibling(part, *rs):
        for r in rs:
            src, dst = pairs(part, 0, r, 1), pairs(part, 1, r, 1)
            links.send(f"{part.tag}to{r}", lambda src=src: t_slots.at[src], lambda dst=dst: t_slots.at[dst], sibling)

    def crossed(part, *rs):
        links.arrived(*(f"{part.tag}to{r}" for r in rs))

    for part in (Y, X, T, U, V):
        part.plan_gather()
        part.plan_sums()
    for part in (T, U, V):
        for r in (2, 0):
            where = sib_rows(part, r, 2)
            links.plan(
                f"{part.tag}back{r}", lambda where=where: t_out.at[where], lambda where=where: t_sib.at[where], sibling
            )

    def back_to_sibling(part):
        for r in (2, 0):
            links.start(f"{part.tag}back{r}")

    def from_sibling(part, r):
        links.arrived(f"{part.tag}back{r}")
        mine = dt[pairs(part, 0, r, 2), :] + t_sib[sib_rows(part, r, 2), :].astype(f32)
        if r == 0:
            t_own[pl.ds(part.first, part.rows), :] = mine[: part.rows]
        t_slots[pairs(part, 0, r, 2), :] = mine.astype(bf16)

    factor, bias = scale_ref[0], bias_ref[0]

    def nothing():
        pass

    def products(text_parts, image_part, first_t, first_i, hooks, texts_first=False):
        tn, n, turns = 16 * text_parts[0].rows, 8 * image_part.rows, len(text_parts)
        i_at = pl.ds(image_part.base, n)

        def image_grads(k, t0):
            g = dot(w_ref[pl.ds(0, tn), pl.ds(0, n)], t_slots[pl.ds(t0, tn), :], 0, 0)
            if not first_i:
                di[i_at, :] += g
            elif turns == 1:
                di[i_at, :] = g
            else:
                di[i_at, :] = jnp.where(k == 0, g, di[i_at, :] + g)

        def text_grads(k, t0):
            d = dot(w_ref[pl.ds(0, tn), pl.ds(0, n)], i_slots[i_at, :], 1, 0)
            if first_t:
                dt[pl.ds(t0, tn), :] = d
            else:
                d = dt[pl.ds(t0, tn), :] + d
                dt[pl.ds(t0, tn // 2), :] = d[: tn // 2]
                out = t0 // 2 if turns == 1 else pl.multiple_of(text_parts[0].base // 2 + k * (tn // 2), 128)
                t_out[pl.ds(out, tn // 2), :] = d[tn // 2 :].astype(bf16)

        def step(k):
            def at_step(calls):
                for turn in range(turns):
                    if calls[turn] is not nothing:
                        calls[turn]() if turns == 1 else pl.when(k == turn)(calls[turn])

            t0 = text_parts[0].base + k * tn
            t0 = t0 if turns == 1 else pl.multiple_of(t0, 128)
            t_at = pl.ds(t0, tn)
            logits = factor * dot(t_slots[t_at, :], i_slots[i_at, :], 1, 1) + bias
            e = jnp.exp(-logits)
            w = 1.0 / (1.0 + e)
            here = where_ref[:, i_at] - t0 == lax.broadcasted_iota(jnp.int32, (tn, n), 0)
            w_ref[pl.ds(0, tn), pl.ds(0, n)] = jnp.where(here, -e * w, w).astype(bf16)
            at_step(hooks[0])
            order = (text_grads, image_grads) if texts_first else (image_grads, text_grads)
            order[0](k, t0)
            at_step(hooks[1])
            order[1](k, t0)
            at_step(hooks[2])

        if turns == 1:
            step(0)
        else:
            pl.loop(0, turns)(step)

    def ready(part, *rs):
        for r in rs:
            where = part.span(r, 0, (0, 2 * part.rows))
            i_sums[where, :] = di[where, :].astype(bf16)

    def each(name, *parts):
        for part in parts:
            getattr(part, name)()

    def steps(*calls):
        def run():
            for call, *args in calls:
                call(*args)

        return run

    each("gather_start", Y, T)
    lane = lax.broadcasted_iota(jnp.int32, (1, IMAGES), 1)
    is_late = lane >= 8 * EARLY
    inner = jnp.where(is_late, lane - 8 * EARLY, lane)
    slot_of = jnp.where(is_late, floor_div(inner, LATE), floor_div(inner, EARLY))
    row_of = inner - slot_of * jnp.where(is_late, LATE, EARLY) + jnp.where(is_late, EARLY, 0)
    pick = (lax.broadcasted_iota(jnp.int32, (ROWS, IMAGES), 0) == row_of).astype(bf16)
    high, low = matches[...] >> 8, matches[...] & 255
    high, low = dot(high.astype(f32).astype(bf16), pick, 1, 0), dot(low.astype(f32).astype(bf16), pick, 1, 0)
    m_slots[0] = high.astype(jnp.int32) * 256 + low.astype(jnp.int32)
    for r in range(4):
        for p in range(2):
            if (r, p) != (0, 0):
                k = ((4 - r) % 4) * 2 + p
                links.send(f"m{k}", lambda: m_slots.at[0], lambda k=k: m_slots.at[k], peers[r, p])
    each("gather_pair", T, Y)
    each("gather_a", T, Y)
    each("gather_b", T, Y)
    U.gather_start()
    T.arrived("gA")
    to_sibling(T, 0)
    each("gather_a2", T, Y)
    each("gather_c", T, Y)
    X.gather_start()
    links.arrived(*(f"m{k}" for k in range(1, 8)))
    match = m_slots[0]
    for k in range(1, 8):
        match = jnp.where(slot_of == k, m_slots[k], match)
    owner = floor_div(match, ROWS)
    row = match - owner * ROWS
    b, g = owner >> 3, owner & 7
    ox = ((b >> 1) & 1) * 2 + (g & 1)
    held = ((g >> 1) == y) & ((ox == x) | (ox == xt))
    slot = jnp.where((b & 1) == core, 0, 8) + (((b >> 2) - z + 4) & 3) * 2 + jnp.where(ox == x, 0, 1)
    spot = jnp.where(row < FIRST, slot * FIRST + row, 16 * FIRST + slot * FIRST + row - FIRST)
    spot = jnp.where(row < 2 * FIRST, spot, 32 * FIRST + slot * LAST + row - 2 * FIRST)
    where_ref[...] = jnp.where(held, spot, -1)

    T.arrived("gD1", "gD3")
    to_sibling(T, 1, 3)
    each("gather_pair", U)
    T.arrived("gB20", "gB21", "gC20", "gC21", "gD2")
    to_sibling(T, 2)
    each("gather_a", U)
    each("gather_b", U)
    V.gather_start()
    Y.arrived("gB20", "gB21", "gC20", "gC21", "gD2", "gA", "gD1", "gD3")
    crossed(T, 0, 1, 3, 2)

    def finish_texts(part):
        rows = pl.ds(part.first, part.rows)
        total = part.total(t_own[rows, :])
        text_grad[rows, :] = norm_back(texts[rows, :], factor * total)

    def finish_images(part):
        rows = pl.ds(part.first, part.rows)
        total = part.total(di[pl.ds(part.base, part.rows), :])
        image_grad[rows, :] = norm_back(images[rows, :], factor * total)

    products((T, U), Y, True, True, (
        (
            steps((each, "gather_a2", U), (each, "gather_c", U), (each, "gather_pair", X)),
            steps((each, "gather_a2", X, V), (each, "gather_c", X, V)),
        ),
        (
            steps(
                (U.arrived, "gA", "gD1", "gD3"), (to_sibling, U, 0, 1, 3),
                (U.arrived, "gB20", "gB21", "gC20", "gC21", "gD2"), (to_sibling, U, 2),
                (each, "gather_a", X), (each, "gather_b", X),
                (each, "gather_pair", V), (each, "gather_a", V), (each, "gather_b", V),
            ),
            steps(
                (V.arrived, "gA", "gD1", "gD3"), (to_sibling, V, 0, 1, 3),
                (V.arrived, "gB20", "gB21", "gC20", "gC21", "gD2"), (to_sibling, V, 2),
            ),
        ),
        (steps((crossed, U, 0, 1, 3, 2)), nothing),
    ))
    crossed(V, 0, 1, 3, 2)
    links.finish()
    products((V,), Y, True, False, (
        (nothing,),
        (steps((ready, Y, 2), (Y.sum_far,), (ready, Y, 1, 3, 0), (Y.sum_pair, 1), (Y.sum_pair, 3), (Y.sum_pair, 0)),),
        (nothing,),
    ))
    X.arrived("gB20", "gB21", "gC20", "gC21", "gD2", "gA", "gD1", "gD3")
    products((T, U), X, False, True, (
        (
            nothing,
            steps(
                (from_sibling, T, 2), (T.sum_far,), (from_sibling, T, 0), *((T.sum_pair, r) for r in (1, 3, 0)),
                (Y.sum_near_a, 1), (Y.sum_near_a, 3),
            ),
        ),
        (
            steps((back_to_sibling, T), (Y.sum_far_a,), (Y.sum_near, 1), (Y.sum_near, 3)),
            steps((back_to_sibling, U), (T.sum_far_a,), (T.sum_near, 1), (T.sum_near, 3)),
        ),
        (nothing, steps((T.sum_near_a, 1), (T.sum_near_a, 3), (Y.sum_own_b,))),
    ), texts_first=True)
    products((V,), X, False, False, (
        (steps(
            (from_sibling, U, 2), (U.sum_far,), (from_sibling, U, 0), *((U.sum_pair, r) for r in (1, 3, 0)),
        ),),
        (steps((back_to_sibling, V), (U.sum_far_a,), (U.sum_near, 1), (U.sum_near, 3)),),
        (steps(
            (ready, X, 2), (X.sum_far,), (ready, X, 1, 3, 0), *((X.sum_pair, r) for r in (1, 3, 0)),
            (T.sum_own_b,), (from_sibling, V, 2), (V.sum_far,), (from_sibling, V, 0),
            *((V.sum_pair, r) for r in (1, 3, 0)), (U.sum_near_a, 1), (U.sum_near_a, 3),
        ),),
    ), texts_first=True)
    X.sum_far_a()
    X.sum_near(1)
    X.sum_near(3)
    V.sum_far_a()
    V.sum_near(1)
    V.sum_near(3)
    U.sum_own_b()
    finish_images(Y)
    X.sum_near_a(1)
    X.sum_near_a(3)
    finish_texts(T)
    V.sum_near_a(1)
    V.sum_near_a(3)
    X.sum_own_b()
    V.sum_own_b()
    finish_texts(U)
    finish_images(X)
    finish_texts(V)
    links.finish()


def per_device(images, texts, match, logit_scale, logit_bias):
    vmem = pl.BlockSpec(memory_space=pltpu.VMEM)
    smem = pl.BlockSpec(memory_space=pltpu.SMEM)
    rows = lambda n: pltpu.VMEM((n, WIDTH), bf16)
    return pl.pallas_call(
        kernel,
        out_shape=(pltpu.VMEM((ROWS, WIDTH), f32), pltpu.VMEM((ROWS, WIDTH), f32)),
        in_specs=[vmem, vmem, vmem, smem, smem],
        out_specs=(vmem, vmem),
        scratch_shapes=[
            rows(IMAGES), rows(TEXTS), pltpu.VMEM((8, 1, IMAGES), jnp.int32), pltpu.VMEM((1, IMAGES), jnp.int32),
            pltpu.VMEM((16 * FIRST, 8 * LATE), bf16), pltpu.VMEM((IMAGES, WIDTH), f32), pltpu.VMEM((TEXTS, WIDTH), f32),
            pltpu.VMEM((ROWS, WIDTH), f32), rows(IMAGES), rows(IMAGES), rows(IMAGES), rows(IMAGES), rows(IMAGES),
            pltpu.SemaphoreType.DMA((SEMS,)), pltpu.SemaphoreType.DMA((SEMS,)),
        ],
        compiler_params=pltpu.CompilerParams(collective_id=0, has_side_effects=True, vmem_limit_bytes=60 << 20),
        cost_estimate=pl.CostEstimate(
            flops=6 * IMAGES * TEXTS * WIDTH, bytes_accessed=8 * ROWS * WIDTH, transcendentals=2 * IMAGES * TEXTS
        ),
        name="contrastive",
    )(images, texts, match[None, :], logit_scale, logit_bias)


def solution(mesh):
    rows = P(("blk", "group"), None)
    return jax.shard_map(
        per_device,
        mesh=mesh,
        in_specs=(rows, rows, P(("blk", "group")), P(), P()),
        out_specs=(rows, rows),
        check_vma=False,
    )
```

```python
import jax
import jax.numpy as jnp
from jax import lax
from jax.experimental import pallas as pl
from jax.experimental.pallas import tpu as pltpu
from jax.sharding import PartitionSpec as P

epsilon = 1e-06
MESH = pl.DeviceIdType.MESH
ROWS, WIDTH = 176, 1152
EARLY, LATE = 96, 80
FIRST, LAST = 64, 48
IMAGES, TEXTS = 8 * ROWS, 16 * ROWS
SEMS = 208
bf16, f32 = jnp.bfloat16, jnp.float32


def place():
    b, g = lax.axis_index("blk"), lax.axis_index("group")
    x = lax.rem(b // 2, 2) * 2 + lax.rem(g, 2)
    return x, g // 2, b // 4, lax.rem(b, 2)


def device(x, y, z, core):
    return ((z * 2 + x // 2) * 2 + core, y * 2 + lax.rem(x, 2))


def unit_rows(x):
    values = x.astype(f32)
    scale = lax.rsqrt(jnp.sum(values * values, axis=1, keepdims=True) + epsilon)
    return values * scale, scale


def norm_back(x, grad):
    unit, scale = unit_rows(x)
    inner = jnp.sum(unit * grad, axis=1, keepdims=True)
    return scale * (grad - unit * inner)


class Links:
    def __init__(self, send_sems, recv_sems):
        self.send_sems, self.recv_sems = send_sems, recv_sems
        self.copies, self.started, self.sent = {}, [], 0

    def plan(self, name, src, dst, target):
        self.copies[name] = len(self.copies), src, dst, target

    def copy(self, name):
        k, src, dst, target = self.copies[name]
        return pltpu.make_async_remote_copy(
            src_ref=src(), dst_ref=dst(), send_sem=self.send_sems.at[k], recv_sem=self.recv_sems.at[k],
            device_id=target, device_id_type=MESH,
        )

    def start(self, name):
        self.copy(name).start()
        self.started.append(name)

    def send(self, name, src, dst, target):
        self.plan(name, src, dst, target)
        self.start(name)

    def arrived(self, *names):
        for name in names:
            self.copy(name).wait_recv()

    def finish(self):
        for name in self.started[self.sent :]:
            self.copy(name).wait_send()
        self.sent = len(self.started)


class Part:
    def __init__(self, tag, links, ways, slots, sums, base, first, rows, cut, half_a, half_b, inbox, box):
        self.tag, self.links = tag, links
        self.up, self.down, self.partner = ways
        self.slots, self.sums, self.base, self.first, self.rows = slots, sums, base, first, rows
        self.all, self.a, self.b = (0, rows), (0, cut), (cut, rows)
        self.a0, self.a1 = (0, half_a), (half_a, cut)
        self.halves = tuple(((cut, at), (at, rows)) for at in (half_b, cut + rows - half_b))
        self.inbox, self.box, self.boxes, self.empty = inbox, box, {}, set()

    def span(self, r, p, part):
        return pl.ds(self.base + (r * 2 + p) * self.rows + part[0], part[1] - part[0])

    def at(self, r, p, part):
        return lambda: self.slots.at[self.span(r, p, part)]

    def plan(self, name, part, src, dst, target):
        if part[1] > part[0]:
            self.links.plan(self.tag + name, src, dst, target)
        else:
            self.empty.add(name)

    def give(self, *names):
        for name in names:
            if name not in self.empty:
                self.links.start(self.tag + name)

    def arrived(self, *names):
        self.links.arrived(*(self.tag + n for n in names if n not in self.empty))

    def plan_gather(self):
        up, down, partner, a, b = self.up, self.down, self.partner, self.a, self.b
        moves = [("gB", 0, 0, 0, 1, b, partner), ("gA", 0, 0, 0, 1, a, partner)]
        moves += [(f"gD{r}", r, 0, r, 1, a, partner) for r in (1, 2, 3)]
        for name, p, part in (("gA", 0, a), ("gB", 0, b), ("gC", 1, b)):
            moves += [(name + "3", 0, p, 3, p, part, up), (name + "1", 0, p, 1, p, part, down)]
            half0, half1 = (self.a0, self.a1) if part is a else self.halves[p]
            moves += [(name + "20", 1, p, 2, p, half0, down), (name + "21", 3, p, 2, p, half1, up)]
        for name, r, p, to_r, to_p, part, target in moves:
            self.plan(name, part, self.at(r, p, part), self.at(to_r, to_p, part), target)

    def gather_start(self):
        self.give("gB", "gA3", "gA1", "gB3", "gB1", "gA")

    def gather_pair(self):
        self.arrived("gB")
        self.give("gC3", "gC1")

    def gather_a(self):
        self.arrived("gA1", "gA3")
        self.give("gA20", "gA21", "gD1", "gD3")

    def gather_b(self):
        self.arrived("gB1", "gB3")
        self.give("gB20", "gB21")

    def gather_a2(self):
        self.arrived("gA20", "gA21")
        self.give("gD2")

    def gather_c(self):
        self.arrived("gC1", "gC3")
        self.give("gC20", "gC21")

    def plan_sums(self):
        up, down = self.up, self.down
        moves = [(f"sX{r}", r, 1, self.a, self.partner) for r in range(4)] + [("sXB", 0, 1, self.b, self.partner)]
        moves += [("sHA1", 2, 0, self.a0, up), ("sHA3", 2, 0, self.a1, down)]
        moves += [("sRA1", 1, 0, self.a, up), ("sRA3", 3, 0, self.a, down)]
        for p in (0, 1):
            moves += [(f"sH1{p}", 2, p, self.halves[p][0], up), (f"sH3{p}", 2, p, self.halves[p][1], down)]
            moves += [(f"sR1{p}", 1, p, self.b, up), (f"sR3{p}", 3, p, self.b, down)]
        for name, r, p, part, target in moves:
            src, size = self.span(r, p, part), part[1] - part[0]
            dst = self.boxes[name] = pl.ds(self.box, size)
            self.box += size
            self.plan(name, part, lambda src=src: self.sums.at[src], lambda dst=dst: self.inbox.at[dst], target)

    def got(self, name):
        self.arrived(name)
        return self.inbox[self.boxes[name], :].astype(f32)

    def add(self, r, p, part, *names):
        if part[1] == part[0]:
            return
        where = self.span(r, p, part)
        total = self.sums[where, :].astype(f32)
        for name in names:
            total = total + self.got(name)
        self.sums[where, :] = total.astype(bf16)

    def sum_far(self):
        self.give("sX2", "sH11", "sH31", "sH10", "sH30")

    def sum_far_a(self):
        self.add(2, 0, self.a, "sX2")
        self.give("sHA1", "sHA3")

    def sum_pair(self, r):
        self.give(f"sX{r}")

    def sum_near(self, r):
        for p in (1, 0):
            self.add(r, p, self.halves[p][r // 2], f"sH{r}{p}")
            self.give(f"sR{r}{p}")

    def sum_near_a(self, r):
        half = self.a0 if r == 1 else self.a1
        self.add(r, 0, self.a, f"sX{r}")
        self.add(r, 0, half, f"sHA{r}")
        self.give(f"sRA{r}")

    def sum_own_b(self):
        self.add(0, 1, self.b, "sR11", "sR31")
        self.give("sXB")

    def total(self, own):
        top = self.got("sX0") + self.got("sRA1") + self.got("sRA3")
        bottom = self.got("sR10") + self.got("sR30") + self.got("sXB")
        return own + jnp.concatenate([top, bottom], axis=0)


def floor_div(a, n):
    return ((a.astype(f32) + 0.5) * (1.0 / n)).astype(jnp.int32)


def dot(a, b, ca, cb):
    return lax.dot_general(a, b, (((ca,), (cb,)), ((), ())), preferred_element_type=f32)


def kernel(
    images, texts, matches, scale_ref, bias_ref, image_grad, text_grad,
    i_slots, t_slots, m_slots, where_ref, w_ref, di, dt, t_own, t_out, t_sib, i_sums, i_inbox, t_inbox, send_sems, recv_sems,
):
    x, y, z, core = place()
    odd = lax.rem(x, 2)
    xi = x + 1 - 2 * odd
    xt = lax.rem(x + 3 + 2 * odd, 4)
    y_up, y_down, y_far = lax.rem(y + 1, 4), lax.rem(y + 3, 4), lax.rem(y + 2, 4)
    z_up, z_down = lax.rem(z + 1, 4), lax.rem(z + 3, 4)
    sibling = device(x, y, z, 1 - core)
    peers = {(r, p): device((x, xi)[p], (y, y_up, y_far, y_down)[r], z, core) for r in range(4) for p in range(2)}
    t_ways = device(x, y, z_up, core), device(x, y, z_down, core), device(xt, y, z, core)
    i_ways = peers[1, 0], peers[3, 0], peers[0, 1]

    barrier = pltpu.get_barrier_semaphore()
    greeted = [d for k, d in peers.items() if k != (0, 0)] + [*t_ways, sibling]
    for d in greeted:
        pl.semaphore_signal(barrier, inc=1, device_id=d, device_id_type=MESH)
    unit = unit_rows(images[...])[0].astype(bf16)
    i_slots[pl.ds(0, EARLY), :] = unit[:EARLY]
    i_slots[pl.ds(8 * EARLY, LATE), :] = unit[EARLY:]
    unit = unit_rows(texts[...])[0].astype(bf16)
    t_slots[pl.ds(0, FIRST), :] = unit[:FIRST]
    t_slots[pl.ds(16 * FIRST, FIRST), :] = unit[FIRST : 2 * FIRST]
    t_slots[pl.ds(32 * FIRST, LAST), :] = unit[2 * FIRST :]
    pl.semaphore_wait(barrier, len(greeted))

    links = Links(send_sems, recv_sems)
    Y = Part("Y", links, i_ways, i_slots, i_sums, 0, 0, EARLY, 48, 32, 64, i_inbox, 0)
    X = Part("X", links, i_ways, i_slots, i_sums, 8 * EARLY, EARLY, LATE, 32, 16, 64, i_inbox, 8 * EARLY)
    T = Part("T", links, t_ways, t_slots, t_slots, 0, 0, FIRST, 32, 16, 48, t_inbox, 0)
    U = Part("U", links, t_ways, t_slots, t_slots, 16 * FIRST, FIRST, FIRST, 32, 16, 48, t_inbox, 8 * FIRST)
    V = Part("V", links, t_ways, t_slots, t_slots, 32 * FIRST, 2 * FIRST, LAST, 16, 16, 32, t_inbox, 16 * FIRST)

    def pairs(part, sibs, r, n):
        return pl.ds(part.base + ((4 * sibs + r) * 2) * part.rows, 2 * n * part.rows)

    def sib_rows(part, r, n):
        return pl.ds(part.base // 2 + r * 2 * part.rows, 2 * n * part.rows)

    def to_sibling(part, *rs):
        for r in rs:
            src, dst = pairs(part, 0, r, 1), pairs(part, 1, r, 1)
            links.send(f"{part.tag}to{r}", lambda src=src: t_slots.at[src], lambda dst=dst: t_slots.at[dst], sibling)

    def crossed(part, *rs):
        links.arrived(*(f"{part.tag}to{r}" for r in rs))

    for part in (Y, X, T, U, V):
        part.plan_gather()
        part.plan_sums()
    for part in (T, U, V):
        for r in (2, 0):
            where = sib_rows(part, r, 2)
            links.plan(
                f"{part.tag}back{r}", lambda where=where: t_out.at[where], lambda where=where: t_sib.at[where], sibling
            )

    def back_to_sibling(part):
        for r in (2, 0):
            links.start(f"{part.tag}back{r}")

    def from_sibling(part, r):
        links.arrived(f"{part.tag}back{r}")
        mine = dt[pairs(part, 0, r, 2), :] + t_sib[sib_rows(part, r, 2), :].astype(f32)
        if r == 0:
            t_own[pl.ds(part.first, part.rows), :] = mine[: part.rows]
        t_slots[pairs(part, 0, r, 2), :] = mine.astype(bf16)

    factor, bias = scale_ref[0], bias_ref[0]

    def nothing():
        pass

    def products(text_parts, image_part, first_t, first_i, hooks, texts_first=False):
        tn, n, turns = 16 * text_parts[0].rows, 8 * image_part.rows, len(text_parts)
        i_at = pl.ds(image_part.base, n)

        def image_grads(k, t0):
            g = dot(w_ref[pl.ds(0, tn), pl.ds(0, n)], t_slots[pl.ds(t0, tn), :], 0, 0)
            if not first_i:
                di[i_at, :] += g
            elif turns == 1:
                di[i_at, :] = g
            else:
                di[i_at, :] = jnp.where(k == 0, g, di[i_at, :] + g)

        def text_grads(k, t0):
            d = dot(w_ref[pl.ds(0, tn), pl.ds(0, n)], i_slots[i_at, :], 1, 0)
            if first_t:
                dt[pl.ds(t0, tn), :] = d
            else:
                d = dt[pl.ds(t0, tn), :] + d
                dt[pl.ds(t0, tn // 2), :] = d[: tn // 2]
                out = t0 // 2 if turns == 1 else pl.multiple_of(text_parts[0].base // 2 + k * (tn // 2), 128)
                t_out[pl.ds(out, tn // 2), :] = d[tn // 2 :].astype(bf16)

        def step(k):
            def at_step(calls):
                for turn in range(turns):
                    if calls[turn] is not nothing:
                        calls[turn]() if turns == 1 else pl.when(k == turn)(calls[turn])

            t0 = text_parts[0].base + k * tn
            t0 = t0 if turns == 1 else pl.multiple_of(t0, 128)
            t_at = pl.ds(t0, tn)
            logits = factor * dot(t_slots[t_at, :], i_slots[i_at, :], 1, 1) + bias
            e = jnp.exp(-logits)
            w = 1.0 / (1.0 + e)
            here = where_ref[:, i_at] - t0 == lax.broadcasted_iota(jnp.int32, (tn, n), 0)
            w_ref[pl.ds(0, tn), pl.ds(0, n)] = jnp.where(here, -e * w, w).astype(bf16)
            at_step(hooks[0])
            order = (text_grads, image_grads) if texts_first else (image_grads, text_grads)
            order[0](k, t0)
            at_step(hooks[1])
            order[1](k, t0)
            at_step(hooks[2])

        if turns == 1:
            step(0)
        else:
            pl.loop(0, turns)(step)

    def ready(part, *rs):
        for r in rs:
            where = part.span(r, 0, (0, 2 * part.rows))
            i_sums[where, :] = di[where, :].astype(bf16)

    def each(name, *parts):
        for part in parts:
            getattr(part, name)()

    def steps(*calls):
        def run():
            for call, *args in calls:
                call(*args)

        return run

    each("gather_start", Y, T)
    lane = lax.broadcasted_iota(jnp.int32, (1, IMAGES), 1)
    is_late = lane >= 8 * EARLY
    inner = jnp.where(is_late, lane - 8 * EARLY, lane)
    slot_of = jnp.where(is_late, floor_div(inner, LATE), floor_div(inner, EARLY))
    row_of = inner - slot_of * jnp.where(is_late, LATE, EARLY) + jnp.where(is_late, EARLY, 0)
    pick = (lax.broadcasted_iota(jnp.int32, (ROWS, IMAGES), 0) == row_of).astype(bf16)
    high, low = matches[...] >> 8, matches[...] & 255
    high, low = dot(high.astype(f32).astype(bf16), pick, 1, 0), dot(low.astype(f32).astype(bf16), pick, 1, 0)
    m_slots[0] = high.astype(jnp.int32) * 256 + low.astype(jnp.int32)
    for r in range(4):
        for p in range(2):
            if (r, p) != (0, 0):
                k = ((4 - r) % 4) * 2 + p
                links.send(f"m{k}", lambda: m_slots.at[0], lambda k=k: m_slots.at[k], peers[r, p])
    each("gather_pair", T, Y)
    each("gather_a", T, Y)
    each("gather_b", T, Y)
    U.gather_start()
    T.arrived("gA")
    to_sibling(T, 0)
    each("gather_a2", T, Y)
    each("gather_c", T, Y)
    X.gather_start()
    links.arrived(*(f"m{k}" for k in range(1, 8)))
    match = m_slots[0]
    for k in range(1, 8):
        match = jnp.where(slot_of == k, m_slots[k], match)
    owner = floor_div(match, ROWS)
    row = match - owner * ROWS
    b, g = owner >> 3, owner & 7
    ox = ((b >> 1) & 1) * 2 + (g & 1)
    held = ((g >> 1) == y) & ((ox == x) | (ox == xt))
    slot = jnp.where((b & 1) == core, 0, 8) + (((b >> 2) - z + 4) & 3) * 2 + jnp.where(ox == x, 0, 1)
    spot = jnp.where(row < FIRST, slot * FIRST + row, 16 * FIRST + slot * FIRST + row - FIRST)
    spot = jnp.where(row < 2 * FIRST, spot, 32 * FIRST + slot * LAST + row - 2 * FIRST)
    where_ref[...] = jnp.where(held, spot, -1)

    T.arrived("gD1", "gD3")
    to_sibling(T, 1, 3)
    each("gather_pair", U)
    T.arrived("gB20", "gB21", "gC20", "gC21", "gD2")
    to_sibling(T, 2)
    each("gather_a", U)
    each("gather_b", U)
    V.gather_start()
    Y.arrived("gB20", "gB21", "gC20", "gC21", "gD2", "gA", "gD1", "gD3")
    crossed(T, 0, 1, 3, 2)

    def finish_texts(part):
        rows = pl.ds(part.first, part.rows)
        total = part.total(t_own[rows, :])
        text_grad[rows, :] = norm_back(texts[rows, :], factor * total)

    def finish_images(part):
        rows = pl.ds(part.first, part.rows)
        total = part.total(di[pl.ds(part.base, part.rows), :])
        image_grad[rows, :] = norm_back(images[rows, :], factor * total)

    products((T, U), Y, True, True, (
        (
            steps((each, "gather_a2", U), (each, "gather_c", U), (each, "gather_pair", X)),
            steps((each, "gather_a2", X, V), (each, "gather_c", X, V)),
        ),
        (
            steps(
                (U.arrived, "gA", "gD1", "gD3"), (to_sibling, U, 0, 1, 3),
                (U.arrived, "gB20", "gB21", "gC20", "gC21", "gD2"), (to_sibling, U, 2),
                (each, "gather_a", X), (each, "gather_b", X),
                (each, "gather_pair", V), (each, "gather_a", V), (each, "gather_b", V),
            ),
            steps(
                (V.arrived, "gA", "gD1", "gD3"), (to_sibling, V, 0, 1, 3),
                (V.arrived, "gB20", "gB21", "gC20", "gC21", "gD2"), (to_sibling, V, 2),
            ),
        ),
        (steps((crossed, U, 0, 1, 3, 2)), nothing),
    ))
    crossed(V, 0, 1, 3, 2)
    links.finish()
    products((V,), Y, True, False, (
        (nothing,),
        (steps((ready, Y, 2), (Y.sum_far,), (ready, Y, 1, 3, 0), (Y.sum_pair, 1), (Y.sum_pair, 3), (Y.sum_pair, 0)),),
        (nothing,),
    ))
    X.arrived("gB20", "gB21", "gC20", "gC21", "gD2", "gA", "gD1", "gD3")
    products((T, U), X, False, True, (
        (
            nothing,
            steps(
                (from_sibling, T, 2), (T.sum_far,), (from_sibling, T, 0), *((T.sum_pair, r) for r in (1, 3, 0)),
                (Y.sum_near_a, 1), (Y.sum_near_a, 3),
            ),
        ),
        (
            steps((back_to_sibling, T), (Y.sum_far_a,), (Y.sum_near, 1), (Y.sum_near, 3)),
            steps((back_to_sibling, U), (T.sum_far_a,), (T.sum_near, 1), (T.sum_near, 3)),
        ),
        (nothing, steps((T.sum_near_a, 1), (T.sum_near_a, 3), (Y.sum_own_b,))),
    ), texts_first=True)
    products((V,), X, False, False, (
        (steps(
            (from_sibling, U, 2), (U.sum_far,), (from_sibling, U, 0), *((U.sum_pair, r) for r in (1, 3, 0)),
        ),),
        (steps((back_to_sibling, V), (U.sum_far_a,), (U.sum_near, 1), (U.sum_near, 3)),),
        (steps(
            (ready, X, 2), (X.sum_far,), (ready, X, 1, 3, 0), *((X.sum_pair, r) for r in (1, 3, 0)),
            (T.sum_own_b,), (from_sibling, V, 2), (V.sum_far,), (from_sibling, V, 0),
            *((V.sum_pair, r) for r in (1, 3, 0)), (U.sum_near_a, 1), (U.sum_near_a, 3),
        ),),
    ), texts_first=True)
    X.sum_far_a()
    X.sum_near(1)
    X.sum_near(3)
    V.sum_far_a()
    V.sum_near(1)
    V.sum_near(3)
    U.sum_own_b()
    finish_images(Y)
    X.sum_near_a(1)
    X.sum_near_a(3)
    finish_texts(T)
    V.sum_near_a(1)
    V.sum_near_a(3)
    X.sum_own_b()
    V.sum_own_b()
    finish_texts(U)
    finish_images(X)
    finish_texts(V)
    links.finish()


def per_device(images, texts, match, logit_scale, logit_bias):
    vmem = pl.BlockSpec(memory_space=pltpu.VMEM)
    smem = pl.BlockSpec(memory_space=pltpu.SMEM)
    rows = lambda n: pltpu.VMEM((n, WIDTH), bf16)
    return pl.pallas_call(
        kernel,
        out_shape=(pltpu.VMEM((ROWS, WIDTH), f32), pltpu.VMEM((ROWS, WIDTH), f32)),
        in_specs=[vmem, vmem, vmem, smem, smem],
        out_specs=(vmem, vmem),
        scratch_shapes=[
            rows(IMAGES), rows(TEXTS), pltpu.VMEM((8, 1, IMAGES), jnp.int32), pltpu.VMEM((1, IMAGES), jnp.int32),
            pltpu.VMEM((16 * FIRST, 8 * EARLY), bf16), pltpu.VMEM((IMAGES, WIDTH), f32), pltpu.VMEM((TEXTS, WIDTH), f32),
            pltpu.VMEM((ROWS, WIDTH), f32), rows(IMAGES), rows(IMAGES), rows(IMAGES), rows(IMAGES), rows(IMAGES),
            pltpu.SemaphoreType.DMA((SEMS,)), pltpu.SemaphoreType.DMA((SEMS,)),
        ],
        compiler_params=pltpu.CompilerParams(collective_id=0, has_side_effects=True, vmem_limit_bytes=60 << 20),
        cost_estimate=pl.CostEstimate(
            flops=6 * IMAGES * TEXTS * WIDTH, bytes_accessed=8 * ROWS * WIDTH, transcendentals=2 * IMAGES * TEXTS
        ),
        name="contrastive",
    )(images, texts, match[None, :], logit_scale, logit_bias)


def solution(mesh):
    rows = P(("blk", "group"), None)
    return jax.shard_map(
        per_device,
        mesh=mesh,
        in_specs=(rows, rows, P(("blk", "group")), P(), P()),
        out_specs=(rows, rows),
        check_vma=False,
    )
```
